512 devices in a mesh: dp: 8 (over y, z_hi), expert: 64 (over x, z_lo, core).
Axes of the slice: x: 4, y: 4, z: 16 (z_hi: 2, z_lo: 8; z = z_hi * 8 + z_lo), core: 2. Of those that a mesh axis runs over, the one named last changes fastest.
Arguments:
- tokens: bfloat16 [2048, 3584], P('expert'), may hold values from -6 to 6
- expert_ids: int32 [2048, 8], P('expert'), may hold values from 0 to 63, all different within a row
- router_gates: float32 [2048, 8], P('expert'), may hold values from 0.1 to 0.6
- replica_plan: int32 [64], replicated, may hold values from 0 to 63, each once
- w_gate: bfloat16 [64, 3584, 1024], P('expert', None, 'dp'), may hold values from -0.09375 to 0.09375
- w_up: bfloat16 [64, 3584, 1024], P('expert', None, 'dp'), may hold values from -0.09375 to 0.09375
- w_down: bfloat16 [64, 3584, 1024], P('expert', None, 'dp'), may hold values from -0.1875 to 0.1875
Outputs:
- mixed: bfloat16 [2048, 3584], P('expert', 'dp')
- expert_load: float32 [64], P('expert')
The draws below stay inside these ranges and needn't reach their ends.
Inputs may be any that keep to these rules, and one draw needn't show every extreme that they name: `expert_ids`: each token names 8 different experts. `replica_plan`: each expert is named exactly once.
All inputs are finite; a program needn't handle non-finite values.
Results may differ from the reference program's by a relative error of at most 0.018.
Values may be sent and summed in bfloat16 or wider, within the bound.
A program may use at most 64 MiB of HBM per device.

```python
import jax
import jax.numpy as jnp
from jax import lax

D = 3584
FFH = 1024
TOP = 8
TOK_DEV = 32
CAP = 4
HID_DEV = 128
EXPERTS = 64
TOKENS = 2048
N_DP = 8
N_EXPERT = 64


def levels(rng, extent, split, smallest, top_value):
    def one(axis_at, shards_of):
        draws = jax.random.uniform(jax.random.fold_in(jax.random.fold_in(rng, 6), axis_at), (shards_of,), jnp.float32, smallest / len(split), top_value / len(split))
        return jnp.repeat(jnp.exp(draws), extent[axis_at] // shards_of).reshape((-1,) + (1,) * (len(extent) - axis_at - 1))

    loudness = one(*split[0])
    for cut in split[1:]:
        loudness = loudness * one(*cut)
    return loudness


def different_ones(rng, rows, count, top, lift):
    ranking = jax.random.permutation(jax.random.fold_in(rng, 1), count)
    pull = ranking
    for power in range(3):
        pull = pull * pull // count
    pull = pull * lift // count
    tickets = jax.random.randint(jax.random.fold_in(rng, 2), (rows, count), 0, 4096) + pull
    holders = jax.random.permutation(jax.random.fold_in(rng, 3), rows)[jnp.arange(count) % rows]
    tickets = jnp.where(jnp.arange(rows)[:, None] == holders[None, :], 1 << 14, tickets)
    score = tickets * count + jnp.arange(count)
    return lax.top_k(score.astype(jnp.int32), top)[1].astype(jnp.int32)


def scatter_about(stream_key, shape, deviation, reach, split=(), held_as=jnp.bfloat16):
    gain = levels(stream_key, shape, split, -0.22, 0.18) if split else 1.0
    result = jax.random.normal(stream_key, shape, jnp.float32) * deviation * gain
    return jnp.minimum(jnp.maximum(result, -reach), reach).astype(held_as)


def setup_inputs(seed: int = 0) -> dict:
    streams_of = jax.random.split(jax.random.key(seed), 8)
    tokens = scatter_about(streams_of[0], (TOKENS, D), 1.0, 6.0, ((0, 64),))
    expert_ids = different_ones(streams_of[1], TOKENS, EXPERTS, TOP, 2048)
    router_gates = jnp.clip(0.1 + 0.5 * jax.random.uniform(streams_of[2], (TOKENS, TOP), jnp.float32) ** levels(streams_of[2], (TOKENS, TOP), ((0, 64),), -0.2, 0.2), 0.1, 0.6)
    replica_plan = jax.random.permutation(streams_of[3], EXPERTS).astype(jnp.int32)
    w_gate = scatter_about(streams_of[4], (EXPERTS, D, FFH), D ** -0.5, 0.09375, ((0, 64), (2, 8)))
    w_up = scatter_about(streams_of[5], (EXPERTS, D, FFH), D ** -0.5, 0.09375, ((0, 64), (2, 8)))
    w_down = scatter_about(streams_of[6], (EXPERTS, D, FFH), FFH ** -0.5, 0.1875, ((0, 64), (2, 8)))
    return {"tokens": tokens, "expert_ids": expert_ids, "router_gates": router_gates, "replica_plan": replica_plan, "w_gate": w_gate, "w_up": w_up, "w_down": w_down}


def slot_layout(grouped, capacity):
    sources = grouped.shape[0]
    tok_rows = grouped.shape[1]
    top_k = grouped.shape[2]
    parity = (jnp.arange(tok_rows, dtype=jnp.int32) % 2)[None, :, None]
    slot_keys = (grouped * 2 + parity).reshape(sources, tok_rows * top_k)
    one_hot = (slot_keys[:, :, None] == jnp.arange(2 * EXPERTS, dtype=jnp.int32)[None, None, :]).astype(jnp.int32)
    running = jnp.cumsum(one_hot, axis=1)
    slot_pos = jnp.sum(running * one_hot, axis=2) - 1
    kept_mask = slot_pos < capacity
    return slot_keys, slot_pos, kept_mask, one_hot


def reference(tokens, expert_ids, router_gates, replica_plan, w_gate, w_up, w_down):
    sources = N_EXPERT
    grouped = expert_ids.reshape(sources, TOK_DEV, TOP)
    slot_keys, slot_pos, kept_mask, one_hot = slot_layout(grouped, CAP)
    expert_of = slot_keys // 2
    parity_of = slot_keys % 2
    source_of = jnp.broadcast_to(jnp.arange(sources, dtype=jnp.int32)[:, None], slot_keys.shape)
    token_of = source_of * TOK_DEV + jnp.arange(TOK_DEV * TOP, dtype=jnp.int32)[None, :] // TOP
    target_pos = jnp.where(kept_mask, slot_pos, CAP)
    table = jnp.full((EXPERTS, sources, 2, CAP), -1, jnp.int32)
    table = table.at[expert_of, source_of, parity_of, target_pos].set(token_of, mode="drop")

    def one_expert(operands):
        table_index, gate_matrix, up_matrix, down_matrix = operands
        flat_index = table_index.reshape(-1)
        picked = tokens[jnp.maximum(flat_index, 0)]
        valid = (flat_index >= 0)[:, None]
        row_block = jnp.where(valid, picked, jnp.zeros_like(picked))
        gate_out = jnp.dot(row_block, gate_matrix, preferred_element_type=jnp.float32)
        up_out = jnp.dot(row_block, up_matrix, preferred_element_type=jnp.float32)
        hidden = (jax.nn.silu(gate_out) * up_out).astype(jnp.bfloat16)
        summed = jnp.zeros((row_block.shape[0], D), jnp.float32)
        for block_number in range(N_DP):
            lower = block_number * HID_DEV
            term = lax.dot_general(hidden[:, lower:lower + HID_DEV], down_matrix[:, lower:lower + HID_DEV],
                                   (((1,), (1,)), ((), ())), preferred_element_type=jnp.float32)
            rounded = lax.optimization_barrier(term.astype(jnp.bfloat16))
            summed = summed + rounded.astype(jnp.float32)
        return summed.astype(jnp.bfloat16)

    results = lax.map(one_expert, (table, w_gate, w_up, w_down)).reshape(EXPERTS, sources, 2, CAP, D)
    gathered = results[expert_of, source_of, parity_of, jnp.minimum(slot_pos, CAP - 1)]
    weighting = router_gates.reshape(sources, TOK_DEV * TOP) * kept_mask.astype(jnp.float32)
    mixed = jnp.sum((weighting[:, :, None] * gathered.astype(jnp.float32)).reshape(sources, TOK_DEV, TOP, D), axis=2)
    mixed = mixed.reshape(TOKENS, D).astype(jnp.bfloat16)
    kept_counts = jnp.sum(one_hot * kept_mask[:, :, None].astype(jnp.int32), axis=(0, 1))
    kept_counts = kept_counts.astype(jnp.float32).reshape(EXPERTS, 2)
    expert_load = (kept_counts[:, 0] + kept_counts[replica_plan, 1]) / (EXPERTS * CAP)
    return mixed, expert_load
```

```python
import jax
import jax.numpy as jnp
from jax import lax
from jax.sharding import PartitionSpec as P


def per_device(tokens, expert_ids, router_gates, replica_plan, w_gate, w_up, w_down):
    tok_rows, top_k = expert_ids.shape
    experts = replica_plan.shape[0]
    capacity = tok_rows // 8
    mine = lax.axis_index("expert")
    ids_all = lax.all_gather(expert_ids, "expert", tiled=True)
    gates_all = lax.all_gather(router_gates, "expert", tiled=True)
    rows_all = lax.all_gather(tokens, "expert", tiled=True)

    def kept_of(expert):
        hit = jnp.any(ids_all == expert, axis=1).reshape(-1, tok_rows // 2, 2)
        before = jnp.cumsum(hit.astype(jnp.int32), axis=1)
        return hit & (before <= capacity)

    own = kept_of(mine)
    copied = kept_of(replica_plan[mine])
    load = (
        jnp.sum(own[:, :, 0].astype(jnp.float32)) + jnp.sum(copied[:, :, 1].astype(jnp.float32))
    ) / (experts * capacity)
    weight = jnp.sum(jnp.where(ids_all == mine, gates_all, 0.0), axis=1) * own.reshape(-1).astype(
        jnp.float32
    )
    gate_out = jnp.dot(rows_all, w_gate[0], preferred_element_type=jnp.float32)
    up_out = jnp.dot(rows_all, w_up[0], preferred_element_type=jnp.float32)
    hidden = (jax.nn.silu(gate_out) * up_out * weight[:, None]).astype(jnp.bfloat16)
    hidden_all = lax.all_gather(hidden, "dp", axis=1, tiled=True)
    down = lax.all_to_all(w_down[0], "dp", split_axis=0, concat_axis=1, tiled=True)
    partial_value = lax.dot_general(
        hidden_all, down, (((1,), (1,)), ((), ())), preferred_element_type=jnp.float32
    ).astype(jnp.bfloat16)
    mixed = lax.psum_scatter(partial_value, "expert", scatter_dimension=0, tiled=True)
    return mixed, load.reshape(1)


def solution(mesh):
    placed = (
        P("expert", None),
        P("expert", None),
        P("expert", None),
        P(),
        P("expert", None, "dp"),
        P("expert", None, "dp"),
        P("expert", None, "dp"),
    )
    return jax.shard_map(
        per_device,
        mesh=mesh,
        in_specs=placed,
        out_specs=(P("expert", "dp"), P("expert")),
        check_vma=False,
    )
```

```python
import jax
import jax.numpy as jnp
from jax import lax
from jax.experimental import pallas as pl
from jax.experimental.pallas import tpu as pltpu
from jax.sharding import PartitionSpec as P

BF16, F32 = jnp.bfloat16, jnp.float32
ROWS, HALF = 32, 16
D = 3584
WA = 1792
WB = D - WA
EXTRA = 128
CAP = 4
SLABS = 8
QUARTER, EIGHTH, PADDED = 896, 448, 512


def kernel(
    tokens, ids, gates, plan, w_gate, w_up, w_down,
    out, load,
    buf_a, buf_b, wgu, wd, hid, part, xin1, xin2, xr, zin, zout, cnt, cnt_in,
    loc, w_s, w_r, wd_s, wd_r, wf_s, wf_r, ax_s, ax_r, az_s, az_r, bz_s, bz_r, bx_s, bx_r,
    h_s, h_r, x1_s, x1_r, x2_s, x2_r, z_s, z_r, c_s, c_r,
):
    dp = lax.axis_index("dp")
    ex = lax.axis_index("expert")
    y, zh = lax.div(dp, 2), lax.rem(dp, 2)
    x, zl, core = lax.div(ex, 16), lax.rem(lax.div(ex, 2), 8), lax.rem(ex, 2)
    z = zh * 8 + zl

    def at_x(dx):
        return (dp, ex + (lax.rem(x + dx + 4, 4) - x) * 16)

    def at_y(dy):
        return (lax.rem(y + dy, 4) * 2 + zh, ex)

    def at_z(dz):
        new = lax.rem(z + dz + 16, 16)
        return (y * 2 + lax.div(new, 8), ex + (lax.rem(new, 8) - zl) * 2)

    peer = (dp, ex + 1 - 2 * core)

    def send(src, dst, ss, rs, dev):
        pltpu.make_async_remote_copy(
            src_ref=src, dst_ref=dst, send_sem=ss, recv_sem=rs, device_id=dev,
            device_id_type=pl.DeviceIdType.MESH,
        ).start()

    def arrived(ref, sem):
        pltpu.make_async_remote_copy(
            src_ref=ref, dst_ref=ref, send_sem=sem, recv_sem=sem, device_id=peer,
            device_id_type=pl.DeviceIdType.MESH,
        ).wait_recv()

    def sent(ref, sem):
        pltpu.make_async_remote_copy(
            src_ref=ref, dst_ref=ref, send_sem=sem, recv_sem=sem, device_id=peer,
            device_id_type=pl.DeviceIdType.MESH,
        ).wait_send()

    def xs(q):
        return lax.rem(x + (0, 3, 1, 2)[q], 4)

    def label(j):
        return lax.rem(zl + (1 - 2 * lax.rem(j, 2)) * lax.div(j + 1, 2) + 8, 8)

    low, high = pl.ds(0, HALF), pl.ds(HALF, HALF)
    core_lanes = pl.multiple_of(core * 256, 128)

    own_a, own_b = buf_a.at[zl, x], buf_b.at[zl, x]
    local = [
        pltpu.make_async_copy(tokens.at[:, pl.ds(0, WA)], own_a, loc.at[0]),
        pltpu.make_async_copy(tokens.at[:, pl.ds(WA, WB)], own_b.at[:, pl.ds(0, WB)], loc.at[1]),
        pltpu.make_async_copy(w_gate.at[0], wgu.at[:, pl.ds(core_lanes, 128)], loc.at[2]),
        pltpu.make_async_copy(w_up.at[0], wgu.at[:, pl.ds(core_lanes + 128, 128)], loc.at[3]),
        pltpu.make_async_copy(
            w_down.at[y],
            wd.at[:, pl.ds(0, EIGHTH), pl.ds(pl.multiple_of((y * 2 + core) * 128, 128), 128)],
            loc.at[4],
        ),
    ]
    for copy in local:
        copy.start()

    barrier = pltpu.get_barrier_semaphore()
    partners = [at_x(1), at_x(-1), at_z(1), at_z(-1), at_y(1), at_y(2), at_y(3), peer]
    for dev in partners:
        pl.semaphore_signal(barrier, inc=1, device_id=dev, device_id_type=pl.DeviceIdType.MESH)

    expert_lane = lax.broadcasted_iota(jnp.int32, (ROWS, EXTRA), 1)
    expert_lane = jnp.where(expert_lane >= 64, expert_lane - 64, expert_lane)
    chosen = jnp.zeros((ROWS, EXTRA), F32)
    weight = jnp.zeros((ROWS, EXTRA), F32)
    for k in range(8):
        hit = ids[:, k : k + 1] == expert_lane
        chosen = chosen + jnp.where(hit, 1.0, 0.0)
        weight = weight + jnp.where(hit, gates[:, k : k + 1], 0.0)
    row = lax.broadcasted_iota(jnp.int32, (ROWS, ROWS), 0)
    col = lax.broadcasted_iota(jnp.int32, (ROWS, ROWS), 1)
    earlier = ((col < row) & (((row - col) & 1) == 0)).astype(BF16)
    before = jnp.dot(earlier, chosen.astype(BF16), preferred_element_type=F32)
    weight = jnp.where(before < CAP - 0.5, weight, 0.0)
    coarse = weight.astype(BF16)
    fine = (weight - coarse.astype(F32)).astype(BF16)
    lanes = lax.broadcasted_iota(jnp.int32, (ROWS, EXTRA), 1)
    buf_b[zl, x, :, pl.ds(WB, EXTRA)] = jnp.where(
        lanes < 64, coarse.astype(F32), fine.astype(F32)
    ).astype(BF16)
    wd[:, pl.ds(EIGHTH, PADDED - EIGHTH), :] = jnp.zeros((2, PADDED - EIGHTH, 1024), BF16)
    cnt[...] = jnp.zeros_like(cnt)
    local[0].wait()
    local[1].wait()
    pl.semaphore_wait(barrier, len(partners))

    def send_az(jd, q):
        odd = lax.rem(jd, 2) == 1
        up = odd if q < 2 else (odd & (jd != 7))
        way = jnp.where(up, 1, -1)
        ref = buf_a.at[lax.rem(zl - way * (lax.div(jd + 1, 2) - 1) + 8, 8), xs(q)]
        send(ref, ref, az_s.at[jd, q], az_r.at[jd, q], at_z(way))

    def send_bz(jd, up, rows, sem):
        way = 1 if up is True else -1 if up is False else jnp.where(up, 1, -1)
        ref = buf_b.at[lax.rem(zl - way * (lax.div(jd + 1, 2) - 1) + 8, 8), x, rows]
        send(ref, ref, bz_s.at[sem], bz_r.at[sem], at_z(way))

    def send_bx(j):
        ref = buf_b.at[label(j), x]
        send(ref, ref, bx_s.at[j, 0], bx_r.at[j, 0], at_x(1))
        send(ref, ref, bx_s.at[j, 1], bx_r.at[j, 1], at_x(-1))

    whole = pl.ds(0, ROWS)
    send_bz(jnp.int32(1), True, whole, 1)
    send_bz(jnp.int32(2), False, whole, 2)
    send(own_a, own_a, ax_s.at[0], ax_r.at[0], at_x(1))
    send(own_a, own_a, ax_s.at[1], ax_r.at[1], at_x(-1))
    send_bx(jnp.int32(0))
    send_az(jnp.int32(1), 0)
    send_az(jnp.int32(2), 0)
    for i, src in enumerate((w_gate, w_up)):
        dst = wgu.at[:, pl.ds(core_lanes + 128 * i, 128)]
        send(src.at[0], dst, w_s.at[i], w_r.at[i], peer)

    def wd_lanes(row_block, which):
        return wd.at[
            :, pl.ds(0, EIGHTH), pl.ds(pl.multiple_of((row_block * 2 + which) * 128, 128), 128)
        ]

    for k in (1, 2, 3):
        send(
            w_down.at[lax.rem(y + k, 4)], wd_lanes(y, core), wd_s.at[k], wd_r.at[k], at_y(k)
        )

    def gather(j):
        nxt = j + 1

        @pl.when(nxt <= 6)
        def _():
            arrived(buf_b.at[label(nxt), x], bz_r.at[nxt])

            @pl.when(nxt <= 4)
            def _():
                send_bz(nxt + 2, lax.rem(nxt, 2) == 1, whole, nxt + 2)

            @pl.when(nxt == 5)
            def _():
                send_bz(jnp.int32(7), True, low, 7)

            @pl.when(nxt == 6)
            def _():
                send_bz(jnp.int32(7), False, high, 8)

        @pl.when(nxt == 7)
        def _():
            arrived(buf_b.at[label(nxt), x, low], bz_r.at[7])
            arrived(buf_b.at[label(nxt), x, high], bz_r.at[8])

        @pl.when(nxt <= 7)
        def _():
            send_bx(nxt)

        @pl.when(j == 0)
        def _():
            one, two = jnp.int32(1), jnp.int32(2)
            ref = buf_a.at[zl, xs(1)]
            arrived(ref, ax_r.at[0])
            send(ref.at[low], ref.at[low], ax_s.at[2], ax_r.at[2], at_x(1))
            send_az(one, 1)
            send_az(two, 1)
            ref = buf_a.at[zl, xs(2)]
            arrived(ref, ax_r.at[1])
            send(ref.at[high], ref.at[high], ax_s.at[3], ax_r.at[3], at_x(-1))
            send_az(one, 2)
            send_az(two, 2)
            arrived(buf_a.at[zl, xs(3), low], ax_r.at[2])
            arrived(buf_a.at[zl, xs(3), high], ax_r.at[3])
            send_az(one, 3)
            send_az(two, 3)

        @pl.when(j > 0)
        def _():
            for q in range(4):
                arrived(buf_a.at[label(j), xs(q)], az_r.at[j, q])
                onward = (j <= 4) | (j == 5 if q < 2 else j == 6)

                @pl.when(onward)
                def _():
                    send_az(jnp.minimum(j + 2, 7), q)

        ref = buf_b.at[label(j), xs(1)]
        arrived(ref, bx_r.at[j, 0])
        send(ref.at[low], ref.at[low], bx_s.at[j, 2], bx_r.at[j, 2], at_x(1))
        ref = buf_b.at[label(j), xs(2)]
        arrived(ref, bx_r.at[j, 1])
        send(ref.at[high], ref.at[high], bx_s.at[j, 3], bx_r.at[j, 3], at_x(-1))
        arrived(buf_b.at[label(j), xs(3), low], bx_r.at[j, 2])
        arrived(buf_b.at[label(j), xs(3), high], bx_r.at[j, 3])

    def experts(j):
        @pl.when(j == 0)
        def _():
            local[2].wait()
            local[3].wait()
            other = pl.multiple_of((1 - core) * 256, 128)
            for i in range(2):
                arrived(wgu.at[:, pl.ds(other + 128 * i, 128)], w_r.at[i])

        slab = label(j)
        acc = jnp.dot(
            buf_a[slab].reshape(128, WA), wgu[pl.ds(0, WA), :], preferred_element_type=F32
        )
        acc = acc + jnp.dot(
            buf_b[slab, :, :, pl.ds(0, WB)].reshape(128, WB),
            wgu[pl.ds(WA, WB), :],
            preferred_element_type=F32,
        )
        mix = buf_b[slab, :, :, pl.ds(WB, EXTRA)].reshape(128, EXTRA)
        lane = lax.broadcasted_iota(jnp.int32, (EXTRA, 256), 0)
        unit = lax.broadcasted_iota(jnp.int32, (EXTRA, 256), 1)
        wanted = (ex - core) + (unit >= 128).astype(jnp.int32)
        pick = ((lane == wanted) | (lane == wanted + 64)).astype(BF16)
        scale = jnp.dot(mix, pick, preferred_element_type=F32)
        gate_out = jnp.concatenate([acc[:, 0:128], acc[:, 256:384]], axis=1)
        up_out = jnp.concatenate([acc[:, 128:256], acc[:, 384:512]], axis=1)
        hidden = gate_out / (1.0 + jnp.exp(-gate_out)) * up_out * scale
        hid[slab, y] = hidden.astype(BF16)
        for k in (1, 2, 3):
            ref = hid.at[slab, y]
            send(ref, ref, h_s.at[j, k], h_r.at[j, k], at_y(k))
        kept = jnp.where(mix.astype(F32) > 0.0, 1.0, 0.0).astype(BF16)
        r = lax.broadcasted_iota(jnp.int32, (8, 128), 0)
        t = lax.broadcasted_iota(jnp.int32, (8, 128), 1)
        parity = (r == (t & 1)).astype(BF16)
        cnt[...] += jnp.dot(parity, kept, preferred_element_type=F32)

        @pl.when(j == 0)
        def _():
            local[4].wait()
            ref = wd_lanes(y, core)
            send(ref, ref, wf_s.at[0], wf_r.at[0], peer)
            for k in (1, 2, 3):
                ref = wd_lanes(lax.rem(y - k + 4, 4), core)
                arrived(ref, wd_r.at[k])
                send(ref, ref, wf_s.at[k], wf_r.at[k], peer)

    def down(j):
        @pl.when(j == 0)
        def _():
            for k in range(4):
                arrived(wd_lanes(lax.rem(y - k + 4, 4), 1 - core), wf_r.at[k])

        slab = label(j)
        for k in (1, 2, 3):
            arrived(hid.at[slab, lax.rem(y - k + 4, 4)], h_r.at[j, k])
        joined = jnp.concatenate([hid[slab, i] for i in range(4)], axis=1)
        for side in range(2):
            value = lax.dot_general(
                joined, wd[side], (((1,), (1,)), ((), ())), preferred_element_type=F32
            )
            part[slab, side] = value.astype(BF16).reshape(4, ROWS, PADDED)
        far = part.at[slab, :, xs(3)]
        send(far.at[:, low], xin1.at[j, 0], x1_s.at[j, 0], x1_r.at[j, 0], at_x(1))
        send(far.at[:, high], xin1.at[j, 1], x1_s.at[j, 1], x1_r.at[j, 1], at_x(-1))

    def add_far(j):
        slab = label(j)
        for i, (q, rows, step) in enumerate(((2, low, 1), (1, high, -1))):
            arrived(xin1.at[j, i], x1_r.at[j, i])
            there = part[slab, :, xs(q), rows, :].astype(F32) + xin1[j, i].astype(F32)
            part[slab, :, xs(q), rows, :] = there.astype(BF16)
            send(part.at[slab, :, xs(q)], xin2.at[j, i], x2_s.at[j, i], x2_r.at[j, i], at_x(step))

    def z_step(s, way, side, first=False, second=False):
        slab = lax.rem(zl - s * way + 8, 8)
        half = lax.div(lax.rem(z + way * (8 - s) + 16, 16), 8)
        value = xr[slab, half]
        rows = low if side == 0 else high
        if first:
            zout[side, s] = value.astype(BF16)
            send(
                zout.at[side, s, rows], zin.at[side, s, rows],
                z_s.at[side, s], z_r.at[side, s], at_z(way),
            )
            return
        if second:
            arrived(zin.at[side, s - 1, rows], z_r.at[side, s - 1])
            zout[side, s] = value.astype(BF16)
            more = xr[slab, half, rows, :] + zin[side, s - 1, rows, :].astype(F32)
            zout[side, s, rows, :] = more.astype(BF16)
        else:
            arrived(zin.at[side, s - 1], z_r.at[side, s - 1])
            zout[side, s] = (value + zin[side, s - 1].astype(F32)).astype(BF16)
        send(zout.at[side, s], zin.at[side, s], z_s.at[side, s], z_r.at[side, s], at_z(way))

    def add_near(j):
        slab = label(j)
        arrived(xin2.at[j, 0], x2_r.at[j, 0])
        arrived(xin2.at[j, 1], x2_r.at[j, 1])
        xr[slab] = (
            part[slab, :, x].astype(F32) + xin2[j, 0].astype(F32) + xin2[j, 1].astype(F32)
        )

        @pl.when(j == 0)
        def _():
            z_step(0, 1, 0, first=True)
            z_step(0, -1, 1, first=True)

        @pl.when(j == 1)
        def _():
            z_step(1, 1, 0, second=True)

        @pl.when(j == 2)
        def _():
            z_step(1, -1, 1, second=True)

        @pl.when((j >= 3) & (lax.rem(j, 2) == 1))
        def _():
            z_step(lax.div(j + 1, 2), 1, 0)

        @pl.when((j >= 3) & ((lax.rem(j, 2) == 0) | (j == 7)))
        def _():
            z_step(lax.div(j + 1, 2), -1, 1)

    def turn(i, carry):
        @pl.when(i < SLABS)
        def _():
            gather(i)

        @pl.when(i >= 3)
        def _():
            add_near(i - 3)

        @pl.when((i >= 2) & (i < SLABS + 2))
        def _():
            add_far(i - 2)

        @pl.when((i >= 1) & (i < SLABS + 1))
        def _():
            down(i - 1)

        @pl.when(i < SLABS)
        def _():
            experts(i)

        @pl.when(i == SLABS)
        def _():
            send(cnt, cnt_in, c_s, c_r, peer)

        return carry

    lax.fori_loop(0, SLABS + 3, turn, 0)

    def last(s, carry):
        z_step(s, 1, 0)
        z_step(s, -1, 1)
        return carry

    lax.fori_loop(5, 8, last, 0)

    arrived(cnt_in, c_r)
    total = cnt[...] + cnt_in[...]
    r = lax.broadcasted_iota(jnp.int32, (8, 128), 0)
    t = lax.broadcasted_iota(jnp.int32, (8, 128), 1)
    copied = plan[ex]
    served = ((r == 0) & (t == ex)) | ((r == 1) & (t == copied))
    amount = jnp.sum(jnp.where(served, total, 0.0), axis=1, keepdims=True)
    amount = jnp.sum(amount, axis=0, keepdims=True) * (1.0 / 256.0)
    load[...] = jnp.broadcast_to(amount, (8, 128))

    arrived(zin.at[0, 7], z_r.at[0, 7])
    arrived(zin.at[1, 7], z_r.at[1, 7])
    mixed = xr[zl, zh] + zin[0, 7].astype(F32) + zin[1, 7].astype(F32)
    out[...] = mixed[:, 0:EIGHTH].astype(BF16)

    block_a, block_b = buf_a.at[0, 0], buf_b.at[0, 0]
    sent(block_a, ax_s.at[0])
    sent(block_a, ax_s.at[1])
    sent(block_a.at[low], ax_s.at[2])
    sent(block_a.at[low], ax_s.at[3])
    sent(block_b.at[low], bz_s.at[7])
    sent(block_b.at[low], bz_s.at[8])
    sent(w_gate.at[0], w_s.at[0])
    sent(w_up.at[0], w_s.at[1])
    sent(cnt, c_s)
    sent(wd_lanes(0, 0), wf_s.at[0])
    for k in (1, 2, 3):
        sent(w_down.at[0], wd_s.at[k])
        sent(wd_lanes(0, 0), wf_s.at[k])
    for side in range(2):
        sent(zout.at[side, 0, low], z_s.at[side, 0])

    def drain(j, carry):
        sent(block_b, bx_s.at[j, 0])
        sent(block_b, bx_s.at[j, 1])
        sent(block_b.at[low], bx_s.at[j, 2])
        sent(block_b.at[low], bx_s.at[j, 3])
        for k in (1, 2, 3):
            sent(hid.at[0, 0], h_s.at[j, k])
        for i in range(2):
            sent(xin1.at[0, 0], x1_s.at[j, i])
            sent(xin2.at[0, 0], x2_s.at[j, i])

        @pl.when(j >= 1)
        def _():
            for q in range(4):
                sent(block_a, az_s.at[j, q])
            for side in range(2):
                sent(zout.at[0, 0], z_s.at[side, j])

        @pl.when((j >= 1) & (j <= 6))
        def _():
            sent(block_b, bz_s.at[j])

        return carry

    lax.fori_loop(0, SLABS, drain, 0)


def per_device(tokens, expert_ids, router_gates, replica_plan, w_gate, w_up, w_down):
    anywhere = pl.BlockSpec(memory_space=pl.ANY)
    vmem = pl.BlockSpec(memory_space=pltpu.VMEM)
    sem = pltpu.SemaphoreType.DMA
    mixed, load = pl.pallas_call(
        kernel,
        out_shape=(
            jax.ShapeDtypeStruct((ROWS, EIGHTH), BF16),
            jax.ShapeDtypeStruct((8, 128), F32),
        ),
        in_specs=[
            anywhere, vmem, vmem, pl.BlockSpec(memory_space=pltpu.SMEM),
            anywhere, anywhere, anywhere,
        ],
        out_specs=(vmem, vmem),
        scratch_shapes=[
            pltpu.VMEM((8, 4, ROWS, WA), BF16),
            pltpu.VMEM((8, 4, ROWS, WB + EXTRA), BF16),
            pltpu.VMEM((D, 512), BF16),
            pltpu.VMEM((2, PADDED, 1024), BF16),
            pltpu.VMEM((8, 4, 128, 256), BF16),
            pltpu.VMEM((8, 2, 4, ROWS, PADDED), BF16),
            pltpu.VMEM((8, 2, 2, HALF, PADDED), BF16),
            pltpu.VMEM((8, 2, 2, ROWS, PADDED), BF16),
            pltpu.VMEM((8, 2, ROWS, PADDED), F32),
            pltpu.VMEM((2, 8, ROWS, PADDED), BF16),
            pltpu.VMEM((2, 8, ROWS, PADDED), BF16),
            pltpu.VMEM((8, 128), F32),
            pltpu.VMEM((8, 128), F32),
            sem((5,)),
            sem((2,)), sem((2,)),
            sem((4,)), sem((4,)),
            sem((4,)), sem((4,)),
            sem((4,)), sem((4,)),
            sem((8, 4)), sem((8, 4)),
            sem((9,)), sem((9,)),
            sem((8, 4)), sem((8, 4)),
            sem((8, 4)), sem((8, 4)),
            sem((8, 2)), sem((8, 2)),
            sem((8, 2)), sem((8, 2)),
            sem((2, 8)), sem((2, 8)),
            sem, sem,
        ],
        compiler_params=pltpu.CompilerParams(
            collective_id=0, has_side_effects=True, vmem_limit_bytes=48 * 1024 * 1024
        ),
        cost_estimate=pl.CostEstimate(
            flops=6_000_000_000, bytes_accessed=4_000_000, transcendentals=300_000
        ),
    )(
        tokens,
        expert_ids,
        router_gates,
        replica_plan,
        w_gate,
        w_up,
        w_down.reshape(4, 2, EIGHTH, 128),
    )
    return mixed, load[0, 0:1]


def solution(mesh):
    placed = (
        P("expert", None),
        P("expert", None),
        P("expert", None),
        P(),
        P("expert", None, "dp"),
        P("expert", None, "dp"),
        P("expert", None, "dp"),
    )
    return jax.shard_map(
        per_device,
        mesh=mesh,
        in_specs=placed,
        out_specs=(P("expert", "dp"), P("expert")),
        check_vma=False,
    )
```

```python
import jax
import jax.numpy as jnp
from jax import lax
from jax.experimental import pallas as pl
from jax.experimental.pallas import tpu as pltpu
from jax.sharding import PartitionSpec as P

BF16, F32 = jnp.bfloat16, jnp.float32
ROWS, HALF = 32, 16
D = 3584
WA = 1792
WB = D - WA
EXTRA = 128
CAP = 4
SLABS = 8
QUARTER, EIGHTH, PADDED = 896, 448, 512


def kernel(
    tokens, ids, gates, plan, w_gate, w_up, w_down,
    out, load,
    buf_a, buf_b, wgu, wd, hid, part, xin1, xin2, xin3, xr, zin, zout, cnt, cnt_in,
    loc, w_s, w_r, wd_s, wd_r, wf_s, wf_r, ax_s, ax_r, az_s, az_r, bz_s, bz_r, bx_s, bx_r,
    h_s, h_r, x1_s, x1_r, x2_s, x2_r, z_s, z_r, c_s, c_r,
):
    dp = lax.axis_index("dp")
    ex = lax.axis_index("expert")
    y, zh = lax.div(dp, 2), lax.rem(dp, 2)
    x, zl, core = lax.div(ex, 16), lax.rem(lax.div(ex, 2), 8), lax.rem(ex, 2)
    z = zh * 8 + zl

    def at_x(dx):
        return (dp, ex + (lax.rem(x + dx + 4, 4) - x) * 16)

    def at_y(dy):
        return (lax.rem(y + dy, 4) * 2 + zh, ex)

    def at_z(dz):
        new = lax.rem(z + dz + 16, 16)
        return (y * 2 + lax.div(new, 8), ex + (lax.rem(new, 8) - zl) * 2)

    peer = (dp, ex + 1 - 2 * core)

    def send(src, dst, ss, rs, dev):
        pltpu.make_async_remote_copy(
            src_ref=src, dst_ref=dst, send_sem=ss, recv_sem=rs, device_id=dev,
            device_id_type=pl.DeviceIdType.MESH,
        ).start()

    def arrived(ref, sem):
        pltpu.make_async_remote_copy(
            src_ref=ref, dst_ref=ref, send_sem=sem, recv_sem=sem, device_id=peer,
            device_id_type=pl.DeviceIdType.MESH,
        ).wait_recv()

    def sent(ref, sem):
        pltpu.make_async_remote_copy(
            src_ref=ref, dst_ref=ref, send_sem=sem, recv_sem=sem, device_id=peer,
            device_id_type=pl.DeviceIdType.MESH,
        ).wait_send()

    def xs(q):
        return lax.rem(x + (0, 3, 1, 2)[q], 4)

    def label(j):
        return lax.rem(zl + (1 - 2 * lax.rem(j, 2)) * lax.div(j + 1, 2) + 8, 8)

    low, high = pl.ds(0, HALF), pl.ds(HALF, HALF)
    core_lanes = pl.multiple_of(core * 256, 128)

    own_a, own_b = buf_a.at[zl, x], buf_b.at[zl, x]
    local = [
        pltpu.make_async_copy(tokens.at[:, pl.ds(0, WA)], own_a, loc.at[0]),
        pltpu.make_async_copy(tokens.at[:, pl.ds(WA, WB)], own_b.at[:, pl.ds(0, WB)], loc.at[1]),
        pltpu.make_async_copy(w_gate.at[0], wgu.at[:, pl.ds(core_lanes, 128)], loc.at[2]),
        pltpu.make_async_copy(w_up.at[0], wgu.at[:, pl.ds(core_lanes + 128, 128)], loc.at[3]),
        pltpu.make_async_copy(
            w_down.at[y],
            wd.at[:, pl.ds(0, EIGHTH), pl.ds(pl.multiple_of((y * 2 + core) * 128, 128), 128)],
            loc.at[4],
        ),
    ]
    for copy in local:
        copy.start()

    barrier = pltpu.get_barrier_semaphore()
    partners = [at_x(1), at_x(-1), at_x(2)]
    partners += [at_z(step) for step in (1, -1, 2, -2, 3, -3, 4, -4)]
    partners += [at_y(1), at_y(2), at_y(3), peer]
    for dev in partners:
        pl.semaphore_signal(barrier, inc=1, device_id=dev, device_id_type=pl.DeviceIdType.MESH)

    wd[:, pl.ds(EIGHTH, PADDED - EIGHTH), :] = jnp.zeros((2, PADDED - EIGHTH, 1024), BF16)
    cnt[...] = jnp.zeros_like(cnt)
    local[0].wait()
    pl.semaphore_wait(barrier, len(partners))

    def send_az(jd, q):
        odd = lax.rem(jd, 2) == 1
        up = odd if q < 2 else (odd & (jd != 7))
        way = jnp.where(up, 1, -1)
        ref = buf_a.at[lax.rem(zl - way * (lax.div(jd + 1, 2) - 1) + 8, 8), xs(q)]
        send(ref, ref, az_s, az_r.at[jd, q], at_z(way))

    def send_bz(jd, up, rows, sem):
        way = 1 if up is True else -1 if up is False else jnp.where(up, 1, -1)
        ref = buf_b.at[lax.rem(zl - way * (lax.div(jd + 1, 2) - 1) + 8, 8), x, rows]
        send(ref, ref, bz_s.at[sem], bz_r.at[sem], at_z(way))

    def send_bx(j):
        ref = buf_b.at[label(j), x]
        send(ref, ref, bx_s, bx_r.at[j, 0], at_x(1))
        send(ref, ref, bx_s, bx_r.at[j, 1], at_x(-1))

    whole = pl.ds(0, ROWS)
    send(own_a, own_a, ax_s.at[0], ax_r.at[0], at_x(1))
    send(own_a, own_a, ax_s.at[1], ax_r.at[1], at_x(-1))
    send_az(jnp.int32(1), 0)
    send_az(jnp.int32(2), 0)
    for i, src in enumerate((w_gate, w_up)):
        dst = wgu.at[:, pl.ds(core_lanes + 128 * i, 128)]
        send(src.at[0], dst, w_s.at[i], w_r.at[i], peer)

    def wd_lanes(row_block, which):
        return wd.at[
            :, pl.ds(0, EIGHTH), pl.ds(pl.multiple_of((row_block * 2 + which) * 128, 128), 128)
        ]

    for k in (1, 2, 3):
        send(
            w_down.at[lax.rem(y + k, 4)], wd_lanes(y, core), wd_s.at[k], wd_r.at[k], at_y(k)
        )

    part_row = lax.broadcasted_iota(jnp.int32, (EXTRA, ROWS), 0)
    expert_row = jnp.where(part_row >= 64, part_row - 64, part_row)
    chosen = jnp.zeros((EXTRA, ROWS), F32)
    weight = jnp.zeros((EXTRA, ROWS), F32)
    for k in range(8):
        hit = ids[k : k + 1, :] == expert_row
        chosen = chosen + jnp.where(hit, 1.0, 0.0)
        weight = weight + jnp.where(hit, gates[k : k + 1, :], 0.0)
    row = lax.broadcasted_iota(jnp.int32, (ROWS, ROWS), 0)
    col = lax.broadcasted_iota(jnp.int32, (ROWS, ROWS), 1)
    earlier = ((row < col) & (((col - row) & 1) == 0)).astype(BF16)
    before = jnp.dot(chosen.astype(BF16), earlier, preferred_element_type=F32)
    weight = jnp.where(before < CAP - 0.5, weight, 0.0)
    coarse = weight.astype(BF16).astype(F32)
    parts = jnp.where(part_row < 64, coarse, weight - coarse).astype(BF16)
    buf_b[zl, x, :, pl.ds(WB, EXTRA)] = lax.dot_general(
        (row == col).astype(BF16), parts, (((1,), (1,)), ((), ())), preferred_element_type=F32
    ).astype(BF16)
    local[1].wait()
    send_bz(jnp.int32(1), True, whole, 1)
    send_bz(jnp.int32(2), False, whole, 2)
    send_bx(jnp.int32(0))

    def first_x():
        one, two = jnp.int32(1), jnp.int32(2)
        ref = buf_a.at[zl, xs(1)]
        arrived(ref, ax_r.at[0])
        send(ref.at[low], ref.at[low], ax_s.at[2], ax_r.at[2], at_x(1))
        send_az(one, 1)
        send_az(two, 1)
        ref = buf_a.at[zl, xs(2)]
        arrived(ref, ax_r.at[1])
        send(ref.at[high], ref.at[high], ax_s.at[3], ax_r.at[3], at_x(-1))
        send_az(one, 2)
        send_az(two, 2)
        arrived(buf_a.at[zl, xs(3), low], ax_r.at[2])
        arrived(buf_a.at[zl, xs(3), high], ax_r.at[3])
        send_az(one, 3)
        send_az(two, 3)

    def along_z(d, q):
        @pl.when((d <= 3) | (q < 2))
        def _():
            jd = 2 * d - 1
            arrived(buf_a.at[label(jd), xs(q)], az_r.at[jd, q])

            @pl.when((d <= 2) | ((d == 3) & (q < 2)))
            def _():
                send_az(jd + 2, q)

        @pl.when((d <= 3) | (q >= 2))
        def _():
            jd = jnp.minimum(2 * d, 7)
            arrived(buf_a.at[label(jd), xs(q)], az_r.at[jd, q])

            @pl.when((d <= 2) | ((d == 3) & (q >= 2)))
            def _():
                send_az(jnp.minimum(jd + 2, 7), q)

    def ahead_z(dist, up):
        side = 0 if up else 1

        @pl.when(dist <= 3)
        def _():
            jd = 2 * dist - 1 + side
            arrived(buf_b.at[label(jd), x], bz_r.at[jd])

            @pl.when(dist <= 2)
            def _():
                send_bz(jd + 2, up, whole, jd + 2)

            @pl.when(dist == 3)
            def _():
                send_bz(jnp.int32(7), up, low if up else high, 7 + side)

            send_bx(jd)

        @pl.when(dist == 4)
        def _():
            jd = jnp.int32(7)
            arrived(buf_b.at[label(jd), x, low if up else high], bz_r.at[7 + side])
            if not up:
                send_bx(jd)

    def along_x(j):
        ref = buf_b.at[label(j), xs(1)]
        arrived(ref, bx_r.at[j, 0])
        send(ref.at[low], ref.at[low], bx_s, bx_r.at[j, 2], at_x(1))
        ref = buf_b.at[label(j), xs(2)]
        arrived(ref, bx_r.at[j, 1])
        send(ref.at[high], ref.at[high], bx_s, bx_r.at[j, 3], at_x(-1))

    def along_x_far(j):
        arrived(buf_b.at[label(j), xs(3), low], bx_r.at[j, 2])
        arrived(buf_b.at[label(j), xs(3), high], bx_r.at[j, 3])

    def experts(j):
        @pl.when(j == 0)
        def _():
            local[2].wait()
            local[3].wait()
            other = pl.multiple_of((1 - core) * 256, 128)
            for i in range(2):
                arrived(wgu.at[:, pl.ds(other + 128 * i, 128)], w_r.at[i])

        slab = label(j)
        acc = jnp.dot(
            buf_a[slab].reshape(128, WA), wgu[pl.ds(0, WA), :], preferred_element_type=F32
        )
        acc = acc + jnp.dot(
            buf_b[slab, :, :, pl.ds(0, WB)].reshape(128, WB),
            wgu[pl.ds(WA, WB), :],
            preferred_element_type=F32,
        )
        mix = buf_b[slab, :, :, pl.ds(WB, EXTRA)].reshape(128, EXTRA)
        lane = lax.broadcasted_iota(jnp.int32, (EXTRA, 256), 0)
        unit = lax.broadcasted_iota(jnp.int32, (EXTRA, 256), 1)
        wanted = (ex - core) + (unit >= 128).astype(jnp.int32)
        pick = ((lane == wanted) | (lane == wanted + 64)).astype(BF16)
        scale = jnp.dot(mix, pick, preferred_element_type=F32)
        gate_out = jnp.concatenate([acc[:, 0:128], acc[:, 256:384]], axis=1)
        up_out = jnp.concatenate([acc[:, 128:256], acc[:, 384:512]], axis=1)
        hidden = gate_out / (1.0 + jnp.exp(-gate_out)) * up_out * scale
        hid[slab, y] = hidden.astype(BF16)
        for k in (1, 2, 3):
            ref = hid.at[slab, y]
            send(ref, ref, h_s, h_r.at[j, k], at_y(k))
        kept = jnp.where(mix.astype(F32) > 0.0, 1.0, 0.0).astype(BF16)
        r = lax.broadcasted_iota(jnp.int32, (8, 128), 0)
        t = lax.broadcasted_iota(jnp.int32, (8, 128), 1)
        parity = (r == (t & 1)).astype(BF16)
        cnt[...] += jnp.dot(parity, kept, preferred_element_type=F32)

    def pass_down_weights():
        local[4].wait()
        ref = wd_lanes(y, core)
        send(ref, ref, wf_s.at[0], wf_r.at[0], peer)
        for k in (1, 2, 3):
            ref = wd_lanes(lax.rem(y - k + 4, 4), core)
            arrived(ref, wd_r.at[k])
            send(ref, ref, wf_s.at[k], wf_r.at[k], peer)

    def down(j):
        @pl.when(j == 0)
        def _():
            for k in range(4):
                arrived(wd_lanes(lax.rem(y - k + 4, 4), 1 - core), wf_r.at[k])

        slab = label(j)
        for k in (1, 2, 3):
            arrived(hid.at[slab, lax.rem(y - k + 4, 4)], h_r.at[j, k])
        joined = jnp.concatenate([hid[slab, i] for i in range(4)], axis=1)
        for side in range(2):
            value = lax.dot_general(
                joined, wd[side], (((1,), (1,)), ((), ())), preferred_element_type=F32
            )
            part[slab, side] = value.astype(BF16).reshape(4, ROWS, PADDED)
        far = part.at[slab, :, xs(3)]

        @pl.when(j < 7)
        def _():
            send(far.at[:, low], xin1.at[j, 0], x1_s, x1_r.at[j, 0], at_x(1))
            send(far.at[:, high], xin1.at[j, 1], x1_s, x1_r.at[j, 1], at_x(-1))

        @pl.when(j == 7)
        def _():
            send(far, xin3, x1_s, x1_r.at[j, 0], at_x(2))
            send(part.at[slab, :, xs(2)], xin2.at[j, 0], x2_s, x2_r.at[j, 0], at_x(1))
            send(part.at[slab, :, xs(1)], xin2.at[j, 1], x2_s, x2_r.at[j, 1], at_x(-1))

    def add_far(j):
        slab = label(j)
        for i, (q, rows, step) in enumerate(((2, low, 1), (1, high, -1))):
            arrived(xin1.at[j, i], x1_r.at[j, i])
            there = part[slab, :, xs(q), rows, :].astype(F32) + xin1[j, i].astype(F32)
            part[slab, :, xs(q), rows, :] = there.astype(BF16)
            send(part.at[slab, :, xs(q)], xin2.at[j, i], x2_s, x2_r.at[j, i], at_x(step))

    def z_step(s, way, side, kind):
        slab = lax.rem(zl - s * way + 8, 8)
        half = lax.div(lax.rem(z + way * (8 - s) + 16, 16), 8)
        value = xr[slab, half]
        rows = low if side == 0 else high
        if kind == "first":
            zout[side, s] = value.astype(BF16)
            send(
                zout.at[side, s, rows], zin.at[side, s, rows],
                z_s.at[side, s], z_r.at[side, s], at_z(way),
            )
            return
        if kind == "second":
            arrived(zin.at[side, s - 1, rows], z_r.at[side, s - 1])
            zout[side, s] = value.astype(BF16)
            more = xr[slab, half, rows, :] + zin[side, s - 1, rows, :].astype(F32)
            zout[side, s, rows, :] = more.astype(BF16)
        elif kind == "alone":
            zout[side, s] = value.astype(BF16)
        else:
            arrived(zin.at[side, s - 1], z_r.at[side, s - 1])
            zout[side, s] = (value + zin[side, s - 1].astype(F32)).astype(BF16)
        there = at_z(way if kind in ("second", "on") else (8 - s) * way)
        send(zout.at[side, s], zin.at[side, s], z_s.at[side, s], z_r.at[side, s], there)

    def both(s, kind):
        z_step(s, 1, 0, kind)
        z_step(s, -1, 1, kind)

    def add_near(j):
        slab = label(j)
        arrived(xin2.at[j, 0], x2_r.at[j, 0])
        arrived(xin2.at[j, 1], x2_r.at[j, 1])
        xr[slab] = (
            part[slab, :, x].astype(F32) + xin2[j, 0].astype(F32) + xin2[j, 1].astype(F32)
        )

        @pl.when(j == 7)
        def _():
            arrived(xin3, x1_r.at[j, 0])
            xr[slab] = xr[slab] + xin3[...].astype(F32)

    def slabs(d, work):
        def one(j, carry):
            work(j)
            return carry

        lax.fori_loop(jnp.maximum(2 * d - 1, 0), jnp.minimum(2 * d, 7) + 1, one, 0)

    def turn(d, carry):
        @pl.when(d == 0)
        def _():
            first_x()
            ahead_z(jnp.int32(1), True)
            ahead_z(jnp.int32(1), False)

        for q in range(4):

            @pl.when(d >= 1)
            def _():
                along_z(d, q)

            if q == 0:
                along_x(jnp.maximum(2 * d - 1, 0))

            if q == 1:

                @pl.when((d >= 1) & (d <= 3))
                def _():
                    along_x(2 * d)

                @pl.when(d >= 2)
                def _():
                    slabs(d - 2, add_far)

            if q >= 2:

                @pl.when(d <= 2)
                def _():
                    ahead_z(d + 2, q == 2)

            if q == 2:

                @pl.when(d == 1)
                def _():
                    pass_down_weights()

                @pl.when(d == 4)
                def _():
                    slabs(d - 1, down)

            if q == 3:

                @pl.when(d >= 2)
                def _():
                    slabs(d - 2, add_near)

                    @pl.when(d == 2)
                    def _():
                        both(0, "first")

                    @pl.when(d == 3)
                    def _():
                        both(1, "second")
                        both(7, "alone")

                    @pl.when(d == 4)
                    def _():
                        both(2, "on")
                        both(6, "alone")
                        slabs(d - 1, add_far)

                slabs(d, along_x_far)

        slabs(d, experts)

        @pl.when((d >= 1) & (d <= 3))
        def _():
            slabs(d - 1, down)

        return carry

    lax.fori_loop(0, 5, turn, 0)
    send(cnt, cnt_in, c_s, c_r, peer)
    slabs(jnp.int32(3), add_near)
    both(3, "on")
    both(5, "alone")
    down(jnp.int32(7))
    add_near(jnp.int32(7))
    both(4, "straight")

    arrived(cnt_in, c_r)
    total = cnt[...] + cnt_in[...]
    r = lax.broadcasted_iota(jnp.int32, (8, 128), 0)
    t = lax.broadcasted_iota(jnp.int32, (8, 128), 1)
    copied = plan[ex]
    served = ((r == 0) & (t == ex)) | ((r == 1) & (t == copied))
    load[0] = jnp.sum(jnp.where(served, total, 0.0)) * (1.0 / 256.0)

    mixed = xr[zl, zh]
    for step in (7, 6, 5, 4):
        for side in range(2):
            arrived(zin.at[side, step], z_r.at[side, step])
            mixed = mixed + zin[side, step].astype(F32)
    out[...] = mixed[:, 0:EIGHTH].astype(BF16)

    block_a, block_b = buf_a.at[0, 0], buf_b.at[0, 0]
    sent(block_a, ax_s.at[0])
    sent(block_a, ax_s.at[1])
    sent(block_a.at[low], ax_s.at[2])
    sent(block_a.at[low], ax_s.at[3])
    sent(block_b.at[low], bz_s.at[7])
    sent(block_b.at[low], bz_s.at[8])
    for jd in range(1, 7):
        sent(block_b, bz_s.at[jd])
    sent(buf_a.at[pl.ds(0, 7)], az_s)
    sent(buf_b.at[pl.ds(0, 6)], bx_s)
    sent(hid.at[pl.ds(0, 6)], h_s)
    sent(hid.at[pl.ds(0, 2)], x1_s)
    sent(hid.at[pl.ds(0, 4)], x2_s)
    sent(w_gate.at[0], w_s.at[0])
    sent(w_up.at[0], w_s.at[1])
    sent(cnt, c_s)
    sent(wd_lanes(0, 0), wf_s.at[0])
    for k in (1, 2, 3):
        sent(w_down.at[0], wd_s.at[k])
        sent(wd_lanes(0, 0), wf_s.at[k])
    for side in range(2):
        sent(zout.at[side, 0, low], z_s.at[side, 0])
        for step in range(1, 8):
            sent(zout.at[side, step], z_s.at[side, step])


def per_device(tokens, expert_ids, router_gates, replica_plan, w_gate, w_up, w_down):
    hbm = pl.BlockSpec(memory_space=pltpu.HBM)
    smem = pl.BlockSpec(memory_space=pltpu.SMEM)
    vmem = pl.BlockSpec(memory_space=pltpu.VMEM)
    sem = pltpu.SemaphoreType.DMA
    mixed, load = pl.pallas_call(
        kernel,
        out_shape=(
            jax.ShapeDtypeStruct((ROWS, EIGHTH), BF16),
            jax.ShapeDtypeStruct((1,), F32),
        ),
        in_specs=[
            hbm, vmem, vmem, smem, hbm, hbm, hbm,
        ],
        out_specs=(vmem, smem),
        scratch_shapes=[
            pltpu.VMEM((8, 4, ROWS, WA), BF16),
            pltpu.VMEM((8, 4, ROWS, WB + EXTRA), BF16),
            pltpu.VMEM((D, 512), BF16),
            pltpu.VMEM((2, PADDED, 1024), BF16),
            pltpu.VMEM((8, 4, 128, 256), BF16),
            pltpu.VMEM((8, 2, 4, ROWS, PADDED), BF16),
            pltpu.VMEM((8, 2, 2, HALF, PADDED), BF16),
            pltpu.VMEM((8, 2, 2, ROWS, PADDED), BF16),
            pltpu.VMEM((2, ROWS, PADDED), BF16),
            pltpu.VMEM((8, 2, ROWS, PADDED), F32),
            pltpu.VMEM((2, 8, ROWS, PADDED), BF16),
            pltpu.VMEM((2, 8, ROWS, PADDED), BF16),
            pltpu.VMEM((8, 128), F32),
            pltpu.VMEM((8, 128), F32),
            sem((5,)),
            sem((2,)), sem((2,)),
            sem((4,)), sem((4,)),
            sem((4,)), sem((4,)),
            sem((4,)), sem((4,)),
            sem, sem((8, 4)),
            sem((9,)), sem((9,)),
            sem, sem((8, 4)),
            sem, sem((8, 4)),
            sem, sem((8, 2)),
            sem, sem((8, 2)),
            sem((2, 8)), sem((2, 8)),
            sem, sem,
        ],
        compiler_params=pltpu.CompilerParams(
            collective_id=0, has_side_effects=True, vmem_limit_bytes=60 * 1024 * 1024
        ),
        cost_estimate=pl.CostEstimate(
            flops=6_000_000_000, bytes_accessed=4_000_000, transcendentals=300_000
        ),
    )(
        tokens,
        expert_ids.T,
        router_gates.T,
        replica_plan,
        w_gate,
        w_up,
        w_down.reshape(4, 2, EIGHTH, 128),
    )
    return mixed, load


def solution(mesh):
    placed = (
        P("expert", None),
        P("expert", None),
        P("expert", None),
        P(),
        P("expert", None, "dp"),
        P("expert", None, "dp"),
        P("expert", None, "dp"),
    )
    return jax.shard_map(
        per_device,
        mesh=mesh,
        in_specs=placed,
        out_specs=(P("expert", "dp"), P("expert")),
        check_vma=False,
    )
```

```python
import jax
import jax.numpy as jnp
from jax import lax
from jax.experimental import pallas as pl
from jax.experimental.pallas import tpu as pltpu
from jax.sharding import PartitionSpec as P

BF16, F32 = jnp.bfloat16, jnp.float32
ROWS, HALF = 32, 16
D = 3584
WC = 256
WA = 1536
WB = D - WA - 4 * WC
EXTRA = 128
SLOTS = 32
CAP = 4
SLABS = 8
QUARTER, EIGHTH, PADDED = 896, 448, 512


def kernel(
    tokens, ids, gates, plan, w_gate, w_up, w_down,
    out, load,
    buf_a, buf_b, buf_c, wgu, wd, hid, pt, part, xin1, xin2, xin3, xr, zin, zout, cnt, cnt_in,
    loc, w_s, w_r, wd_s, wd_r, wf_s, wf_r, ax_s, ax_r, az_s, az_r, bz_s, bz_r, bx_s, bx_r,
    cc_s, cc_r, h_s, h_r, x1_s, x1_r, x2_s, x2_r, z_s, z_r, c_s, c_r,
):
    dp = lax.axis_index("dp")
    ex = lax.axis_index("expert")
    y, zh = lax.div(dp, 2), lax.rem(dp, 2)
    x, zl, core = lax.div(ex, 16), lax.rem(lax.div(ex, 2), 8), lax.rem(ex, 2)
    z = zh * 8 + zl

    known = {}

    def at_x(dx):
        if ("x", dx) not in known:
            known["x", dx] = (dp, ex + (lax.rem(x + dx + 4, 4) - x) * 16)
        return known["x", dx]

    def at_y(dy):
        if ("y", dy) not in known:
            known["y", dy] = (lax.rem(y + dy, 4) * 2 + zh, ex)
        return known["y", dy]

    def at_z(dz):
        if ("z", dz) not in known:
            new = lax.rem(z + dz + 16, 16)
            known["z", dz] = (y * 2 + lax.div(new, 8), ex + (lax.rem(new, 8) - zl) * 2)
        return known["z", dz]

    peer = (dp, ex + 1 - 2 * core)

    def send(src, dst, ss, rs, dev):
        pltpu.make_async_remote_copy(
            src_ref=src, dst_ref=dst, send_sem=ss, recv_sem=rs, device_id=dev,
            device_id_type=pl.DeviceIdType.MESH,
        ).start()

    def arrived(ref, sem):
        pltpu.make_async_remote_copy(
            src_ref=ref, dst_ref=ref, send_sem=sem, recv_sem=sem, device_id=peer,
            device_id_type=pl.DeviceIdType.MESH,
        ).wait_recv()

    def sent(ref, sem):
        pltpu.make_async_remote_copy(
            src_ref=ref, dst_ref=ref, send_sem=sem, recv_sem=sem, device_id=peer,
            device_id_type=pl.DeviceIdType.MESH,
        ).wait_send()

    blocks = [lax.rem(x + step, 4) for step in (0, 3, 1, 2)]
    quarters = [lax.rem(y - k + 4, 4) for k in range(4)]

    def xs(q):
        return blocks[q]

    def wrap(place):
        place = jnp.where(place < 0, place + 8, place)
        return jnp.where(place >= 8, place - 8, place)

    def label(d, side):
        return wrap(zl + (2 * side - 1) * d)

    def turn_of(d, side):
        return 2 * d - 1 + side

    low, high = pl.ds(0, HALF), pl.ds(HALF, HALF)
    core_lanes = pl.multiple_of(core * 256, 128)

    own_a, own_b = buf_a.at[zl, x], buf_b.at[zl, x]
    local = [
        pltpu.make_async_copy(tokens.at[:, pl.ds(0, WA)], own_a, loc.at[0]),
        pltpu.make_async_copy(tokens.at[:, pl.ds(WA, WB)], own_b.at[:, pl.ds(0, WB)], loc.at[1]),
        pltpu.make_async_copy(w_gate.at[0], wgu.at[:, pl.ds(core_lanes, 128)], loc.at[2]),
        pltpu.make_async_copy(w_up.at[0], wgu.at[:, pl.ds(core_lanes + 128, 128)], loc.at[3]),
        pltpu.make_async_copy(
            w_down.at[y],
            wd.at[:, pl.ds(0, EIGHTH), pl.ds(pl.multiple_of((core * 4 + y) * 128, 128), 128)],
            loc.at[4],
        ),
        pltpu.make_async_copy(
            tokens.at[:, pl.ds(pl.multiple_of(WA + WB + y * WC, 128), WC)],
            own_b.at[:, pl.ds(WB + EXTRA, WC)],
            loc.at[5],
        ),
    ]
    for copy in local:
        copy.start()

    barrier = pltpu.get_barrier_semaphore()
    partners = [at_x(1), at_x(-1), at_x(2)]
    partners += [at_z(step) for step in (1, -1, 2, -2, 3, -3, 4, -4)]
    partners += [at_y(1), at_y(2), at_y(3), peer]
    for dev in partners:
        pl.semaphore_signal(barrier, inc=1, device_id=dev, device_id_type=pl.DeviceIdType.MESH)

    wd[:, pl.ds(EIGHTH, PADDED - EIGHTH), :] = jnp.zeros((2, PADDED - EIGHTH, 1024), BF16)
    cnt[...] = jnp.zeros_like(cnt)
    local[0].wait()
    pl.semaphore_wait(barrier, len(partners))

    def send_az(dist, side, q):
        way = 1 - 2 * side
        ref = buf_a.at[wrap(zl - way * (dist - 1)), xs(q)]
        jd = jnp.minimum(turn_of(dist, side), 7)
        send(ref, ref, az_s, az_r.at[jd, q], at_z(way))

    def send_bz(dist, side, rows, sem):
        way = 1 - 2 * side
        ref = buf_b.at[wrap(zl - way * (dist - 1)), x, rows]
        send(ref, ref, bz_s.at[sem], bz_r.at[sem], at_z(way))

    def send_bx(d, side):
        ref, j = buf_b.at[label(d, side), x], turn_of(d, side)
        send(ref, ref, bx_s, bx_r.at[j, 0], at_x(1))
        send(ref, ref, bx_s, bx_r.at[j, 1], at_x(-1))

    whole = pl.ds(0, ROWS)
    send(own_a, own_a, ax_s.at[0], ax_r.at[0], at_x(1))
    send(own_a, own_a, ax_s.at[1], ax_r.at[1], at_x(-1))
    send_az(1, 0, 0)
    send_az(1, 1, 0)
    for i, src in enumerate((w_gate, w_up)):
        dst = wgu.at[:, pl.ds(core_lanes + 128 * i, 128)]
        send(src.at[0], dst, w_s.at[i], w_r.at[i], peer)

    def wd_lanes(row_block, which):
        return wd.at[
            :, pl.ds(0, EIGHTH), pl.ds(pl.multiple_of((which * 4 + row_block) * 128, 128), 128)
        ]

    for k in (1, 2, 3):
        send(
            w_down.at[lax.rem(y + k, 4)], wd_lanes(y, core), wd_s.at[k], wd_r.at[k], at_y(k)
        )

    part_row = lax.broadcasted_iota(jnp.int32, (EXTRA, ROWS), 0)
    expert_row = jnp.where(part_row >= 64, part_row - 64, part_row)
    chosen = jnp.zeros((EXTRA, ROWS), F32)
    weight = jnp.zeros((EXTRA, ROWS), F32)
    for k in range(8):
        hit = ids[k : k + 1, :] == expert_row
        chosen = chosen + jnp.where(hit, 1.0, 0.0)
        weight = weight + jnp.where(hit, gates[k : k + 1, :], 0.0)
    row = lax.broadcasted_iota(jnp.int32, (ROWS, ROWS), 0)
    col = lax.broadcasted_iota(jnp.int32, (ROWS, ROWS), 1)
    earlier = ((row < col) & (((col - row) & 1) == 0)).astype(BF16)
    before = jnp.dot(chosen.astype(BF16), earlier, preferred_element_type=F32)
    weight = jnp.where(before < CAP - 0.5, weight, 0.0)
    coarse = weight.astype(BF16).astype(F32)
    parts = jnp.where(part_row < 64, coarse, weight - coarse).astype(BF16)
    buf_b[zl, x, :, pl.ds(WB, EXTRA)] = lax.dot_general(
        (row == col).astype(BF16), parts, (((1,), (1,)), ((), ())), preferred_element_type=F32
    ).astype(BF16)
    local[1].wait()
    local[5].wait()
    send_bz(1, 0, whole, 1)
    send_bz(1, 1, whole, 2)
    send_bx(0, 1)

    def first_x():
        ref = buf_a.at[zl, xs(1)]
        arrived(ref, ax_r.at[0])
        send(ref.at[low], ref.at[low], ax_s.at[2], ax_r.at[2], at_x(1))
        send_az(1, 0, 1)
        send_az(1, 1, 1)
        ref = buf_a.at[zl, xs(2)]
        arrived(ref, ax_r.at[1])
        send(ref.at[high], ref.at[high], ax_s.at[3], ax_r.at[3], at_x(-1))
        send_az(1, 0, 2)
        send_az(1, 1, 2)
        arrived(buf_a.at[zl, xs(3), low], ax_r.at[2])
        arrived(buf_a.at[zl, xs(3), high], ax_r.at[3])
        send_az(1, 0, 3)
        send_az(1, 1, 3)

    def along_z(d, q):
        for side in range(2):
            mine = q // 2 == side

            @pl.when((d <= 3) | mine)
            def _():
                jd = jnp.minimum(turn_of(d, side), 7)
                arrived(buf_a.at[label(d, side), xs(q)], az_r.at[jd, q])

                @pl.when((d <= 2) | ((d == 3) & mine))
                def _():
                    send_az(d + 1, side, q)

    def ahead_z(dist, side):
        half = high if side else low

        @pl.when(dist <= 3)
        def _():
            jd = turn_of(dist, side)
            arrived(buf_b.at[label(dist, side), x], bz_r.at[jd])

            @pl.when(dist <= 2)
            def _():
                send_bz(dist + 1, side, whole, jd + 2)

            @pl.when(dist == 3)
            def _():
                send_bz(4, side, half, 7 + side)

            send_bx(dist, side)

        @pl.when(dist == 4)
        def _():
            arrived(buf_b.at[label(4, side), x, half], bz_r.at[7 + side])
            if side:
                send_bx(4, 0)

    def along_x(d, side):
        slab, j = label(d, side), turn_of(d, side)
        ref = buf_b.at[slab, xs(1)]
        arrived(ref, bx_r.at[j, 0])
        send(ref.at[low], ref.at[low], bx_s, bx_r.at[j, 2], at_x(1))
        ref = buf_b.at[slab, xs(2)]
        arrived(ref, bx_r.at[j, 1])
        send(ref.at[high], ref.at[high], bx_s, bx_r.at[j, 3], at_x(-1))

    def along_x_far(d, side):
        slab, j = label(d, side), turn_of(d, side)
        arrived(buf_b.at[slab, xs(3), low], bx_r.at[j, 2])
        arrived(buf_b.at[slab, xs(3), high], bx_r.at[j, 3])
        for k in (1, 2, 3):
            send(
                buf_b.at[slab, :, :, pl.ds(WB + EXTRA, WC)], buf_c.at[slab, y],
                cc_s.at[k], cc_r.at[j, k], at_y(k),
            )

    def experts(d, side):
        slab, j = label(d, side), turn_of(d, side)
        @pl.when(j == 0)
        def _():
            local[2].wait()
            local[3].wait()
            other = pl.multiple_of((1 - core) * 256, 128)
            for i in range(2):
                arrived(wgu.at[:, pl.ds(other + 128 * i, 128)], w_r.at[i])

        acc = jnp.dot(
            buf_a[slab].reshape(128, WA), wgu[pl.ds(0, WA), :], preferred_element_type=F32
        )
        acc = acc + jnp.dot(
            buf_b[slab, :, :, pl.ds(0, WB)].reshape(128, WB),
            wgu[pl.ds(WA, WB), :],
            preferred_element_type=F32,
        )

        def quarter(which):
            return wgu[pl.ds(pl.multiple_of(WA + WB + which * WC, WC), WC), :]

        acc = acc + jnp.dot(
            buf_b[slab, :, :, pl.ds(WB + EXTRA, WC)].reshape(128, WC),
            quarter(y),
            preferred_element_type=F32,
        )
        for k in (1, 2, 3):
            which = quarters[k]
            arrived(buf_c.at[slab, which], cc_r.at[j, k])
            acc = acc + jnp.dot(
                buf_c[slab, which].reshape(128, WC), quarter(which), preferred_element_type=F32
            )
        mix = buf_b[slab, :, :, pl.ds(WB, EXTRA)].reshape(128, EXTRA)
        lane = lax.broadcasted_iota(jnp.int32, (EXTRA, 256), 0)
        unit = lax.broadcasted_iota(jnp.int32, (EXTRA, 256), 1)
        wanted = (ex - core) + (unit >= 128).astype(jnp.int32)
        pick = ((lane == wanted) | (lane == wanted + 64)).astype(BF16)
        scale = jnp.dot(mix, pick, preferred_element_type=F32)
        gate_out = jnp.concatenate([acc[:, 0:128], acc[:, 256:384]], axis=1)
        up_out = jnp.concatenate([acc[:, 128:256], acc[:, 384:512]], axis=1)
        hidden = gate_out / (1.0 + jnp.exp(-gate_out)) * up_out * scale
        hidden = hidden.astype(BF16)
        row = lax.broadcasted_iota(jnp.int32, (128, 128), 0)
        col = lax.broadcasted_iota(jnp.int32, (128, 128), 1)
        earlier = (col < row) & ((row >> 5) == (col >> 5)) & (((row - col) & 1) == 0)
        token = lax.broadcasted_iota(jnp.int32, (128, 256), 0)
        slot = lax.broadcasted_iota(jnp.int32, (128, 256), 1) & 127
        first = ((token >> 5) * 8 + (token & 1) * 4).astype(F32)
        served = jnp.where(scale > 0.0, 1.0, 0.0)
        before = jnp.dot(earlier.astype(BF16), served.astype(BF16), preferred_element_type=F32)
        place = jnp.where(before + first == slot.astype(F32), served, 0.0).astype(BF16)
        pt[slab] = place
        for e in range(2):
            lanes = slice(e * 128, e * 128 + 128)
            packed = lax.dot_general(
                place[:, lanes], hidden[:, lanes], (((0,), (0,)), ((), ())),
                preferred_element_type=F32,
            )
            hid[slab, y, pl.ds(e * SLOTS, SLOTS), :] = packed[0:SLOTS].astype(BF16)
        for k in (1, 2, 3):
            ref = hid.at[slab, y]
            send(ref, ref, h_s, h_r.at[j, k], at_y(k))
        kept = jnp.where(mix.astype(F32) > 0.0, 1.0, 0.0).astype(BF16)
        r = lax.broadcasted_iota(jnp.int32, (8, 128), 0)
        t = lax.broadcasted_iota(jnp.int32, (8, 128), 1)
        parity = (r == (t & 1)).astype(BF16)
        cnt[...] += jnp.dot(parity, kept, preferred_element_type=F32)

    def pass_down_weights():
        local[4].wait()
        ref = wd_lanes(y, core)
        send(ref, ref, wf_s.at[0], wf_r.at[0], peer)
        for k in (1, 2, 3):
            ref = wd_lanes(quarters[k], core)
            arrived(ref, wd_r.at[k])
            send(ref, ref, wf_s.at[k], wf_r.at[k], peer)

    def down(d, side):
        slab, j = label(d, side), turn_of(d, side)
        @pl.when(j == 0)
        def _():
            for k in range(4):
                arrived(wd_lanes(quarters[k], 1 - core), wf_r.at[k])

        for k in (1, 2, 3):
            arrived(hid.at[slab, quarters[k]], h_r.at[j, k])
        spread = []
        for e in range(2):
            rows = pl.ds(e * SLOTS, SLOTS)
            packed = jnp.concatenate([hid[slab, i, rows, :] for i in range(4)], axis=1)
            place = pt[slab, :, pl.ds(e * 128, 128)][:, 0:SLOTS]
            spread.append(jnp.dot(place, packed, preferred_element_type=F32).astype(BF16))
        joined = jnp.concatenate(spread, axis=1)
        for side in range(2):
            value = lax.dot_general(
                joined, wd[side], (((1,), (1,)), ((), ())), preferred_element_type=F32
            )
            part[slab, side] = value.astype(BF16).reshape(4, ROWS, PADDED)
        far = part.at[slab, :, xs(3)]

        @pl.when(j < 7)
        def _():
            send(far.at[:, low], xin1.at[j, 0], x1_s, x1_r.at[j, 0], at_x(1))
            send(far.at[:, high], xin1.at[j, 1], x1_s, x1_r.at[j, 1], at_x(-1))

        @pl.when(j == 7)
        def _():
            send(far, xin3, x1_s, x1_r.at[j, 0], at_x(2))
            send(part.at[slab, :, xs(2)], xin2.at[j, 0], x2_s, x2_r.at[j, 0], at_x(1))
            send(part.at[slab, :, xs(1)], xin2.at[j, 1], x2_s, x2_r.at[j, 1], at_x(-1))

    def add_far(d, side):
        slab, j = label(d, side), turn_of(d, side)
        for i, (q, rows, step) in enumerate(((2, low, 1), (1, high, -1))):
            arrived(xin1.at[j, i], x1_r.at[j, i])
            there = part[slab, :, xs(q), rows, :].astype(F32) + xin1[j, i].astype(F32)
            part[slab, :, xs(q), rows, :] = there.astype(BF16)
            send(part.at[slab, :, xs(q)], xin2.at[j, i], x2_s, x2_r.at[j, i], at_x(step))

    halves = {
        (side, s): lax.div(lax.rem(z + (1 - 2 * side) * (8 - s) + 16, 16), 8)
        for side in range(2)
        for s in range(8)
    }

    def z_step(s, way, side, kind):
        slab = wrap(zl - s * way)
        half = halves[side, s]
        value = xr[slab, half]
        rows = low if side == 0 else high
        if kind == "first":
            zout[side, s] = value.astype(BF16)
            send(
                zout.at[side, s, rows], zin.at[side, s, rows],
                z_s.at[side, s], z_r.at[side, s], at_z(way),
            )
            return
        if kind == "second":
            arrived(zin.at[side, s - 1, rows], z_r.at[side, s - 1])
            zout[side, s] = value.astype(BF16)
            more = xr[slab, half, rows, :] + zin[side, s - 1, rows, :].astype(F32)
            zout[side, s, rows, :] = more.astype(BF16)
        elif kind == "alone":
            zout[side, s] = value.astype(BF16)
        else:
            arrived(zin.at[side, s - 1], z_r.at[side, s - 1])
            zout[side, s] = (value + zin[side, s - 1].astype(F32)).astype(BF16)
        there = at_z(way if kind in ("second", "on") else (8 - s) * way)
        send(zout.at[side, s], zin.at[side, s], z_s.at[side, s], z_r.at[side, s], there)

    def both(s, kind):
        z_step(s, 1, 0, kind)
        z_step(s, -1, 1, kind)

    def add_near(d, side):
        slab, j = label(d, side), turn_of(d, side)
        arrived(xin2.at[j, 0], x2_r.at[j, 0])
        arrived(xin2.at[j, 1], x2_r.at[j, 1])
        xr[slab] = (
            part[slab, :, x].astype(F32) + xin2[j, 0].astype(F32) + xin2[j, 1].astype(F32)
        )

        @pl.when(j == 7)
        def _():
            arrived(xin3, x1_r.at[j, 0])
            xr[slab] = xr[slab] + xin3[...].astype(F32)

    def send_c(j):
        for k in (1, 2, 3):
            send(
                buf_b.at[slab, :, :, pl.ds(WB + EXTRA, WC)], buf_c.at[slab, y],
                cc_s.at[k], cc_r.at[j, k], at_y(k),
            )

    def pair(d, work):
        def one(side, carry):
            work(d, side)
            return carry

        lax.fori_loop(0, 2, one, 0)

    def slabs(d, work, least=0, most=4):
        @pl.when((d >= max(least, 1)) & (d <= most))
        def _():
            work(d, 0)

        @pl.when((d >= least) & (d <= min(most, 3)))
        def _():
            work(d, 1)

    def loop_slabs(d, work):
        def one(side, carry):
            work(d, side)
            return carry

        lax.fori_loop(jnp.where(d == 0, 1, 0), jnp.where(d == 4, 1, 2), one, 0)

    def turn(d, carry):
        @pl.when(d == 0)
        def _():
            first_x()
            ahead_z(1, 0)
            ahead_z(1, 1)

        for q in range(4):

            @pl.when(d >= 1)
            def _():
                along_z(d, q)

            if q == 0:

                @pl.when(d >= 1)
                def _():
                    along_x(d, 0)

            if q == 1:

                @pl.when(d <= 3)
                def _():
                    along_x(d, 1)

            if q >= 2:

                @pl.when(d <= 2)
                def _():
                    ahead_z(d + 2, q - 2)

            if q == 2:

                @pl.when(d >= 1)
                def _():
                    loop_slabs(d - 1, experts)

                @pl.when(d == 1)
                def _():
                    pass_down_weights()

            if q == 3:
                slabs(d, along_x_far)

                @pl.when(d >= 3)
                def _():
                    loop_slabs(d - 3, add_near)

                    @pl.when(d == 3)
                    def _():
                        both(0, "first")

                    @pl.when(d == 4)
                    def _():
                        both(1, "second")
                        both(7, "alone")

                @pl.when(d >= 2)
                def _():
                    loop_slabs(d - 2, add_far)

        @pl.when(d >= 1)
        def _():
            loop_slabs(d - 1, down)

        return carry

    lax.fori_loop(0, 5, turn, 0)
    experts(4, 0)
    send(cnt, cnt_in, c_s, c_r, peer)
    pair(3, add_far)
    pair(2, add_near)
    both(2, "on")
    both(6, "alone")
    down(4, 0)
    pair(3, add_near)
    both(3, "on")
    both(5, "alone")
    add_near(4, 0)
    both(4, "straight")

    arrived(cnt_in, c_r)
    total = cnt[...] + cnt_in[...]
    r = lax.broadcasted_iota(jnp.int32, (8, 128), 0)
    t = lax.broadcasted_iota(jnp.int32, (8, 128), 1)
    copied = plan[ex]
    served = ((r == 0) & (t == ex)) | ((r == 1) & (t == copied))
    load[0] = jnp.sum(jnp.where(served, total, 0.0)) * (1.0 / 256.0)

    mixed = xr[zl, zh]
    for step in (7, 6, 5, 4):
        for side in range(2):
            arrived(zin.at[side, step], z_r.at[side, step])
            mixed = mixed + zin[side, step].astype(F32)
    out[...] = mixed[:, 0:EIGHTH].astype(BF16)

    block_a, block_b = buf_a.at[0, 0], buf_b.at[0, 0]
    sent(block_a, ax_s.at[0])
    sent(block_a, ax_s.at[1])
    sent(block_a.at[low], ax_s.at[2])
    sent(block_a.at[low], ax_s.at[3])
    sent(block_b.at[low], bz_s.at[7])
    sent(block_b.at[low], bz_s.at[8])
    for jd in range(1, 7):
        sent(block_b, bz_s.at[jd])
    sent(buf_a.at[pl.ds(0, 7)], az_s)
    sent(buf_b.at[pl.ds(0, 6)], bx_s)
    sent(wd.at[0, pl.ds(0, 192)], h_s)
    for k in (1, 2, 3):
        sent(wd.at[0, pl.ds(0, WC)], cc_s.at[k])
    sent(wd.at[0, pl.ds(0, 256)], x1_s)
    sent(wd.at[0], x2_s)
    sent(w_gate.at[0], w_s.at[0])
    sent(w_up.at[0], w_s.at[1])
    sent(cnt, c_s)
    sent(wd_lanes(0, 0), wf_s.at[0])
    for k in (1, 2, 3):
        sent(w_down.at[0], wd_s.at[k])
        sent(wd_lanes(0, 0), wf_s.at[k])
    for side in range(2):
        sent(zout.at[side, 0, low], z_s.at[side, 0])
        for step in range(1, 8):
            sent(zout.at[side, step], z_s.at[side, step])


def per_device(tokens, expert_ids, router_gates, replica_plan, w_gate, w_up, w_down):
    hbm = pl.BlockSpec(memory_space=pltpu.HBM)
    smem = pl.BlockSpec(memory_space=pltpu.SMEM)
    vmem = pl.BlockSpec(memory_space=pltpu.VMEM)
    sem = pltpu.SemaphoreType.DMA
    mixed, load = pl.pallas_call(
        kernel,
        out_shape=(
            jax.ShapeDtypeStruct((ROWS, EIGHTH), BF16),
            jax.ShapeDtypeStruct((1,), F32),
        ),
        in_specs=[
            hbm, vmem, vmem, smem, hbm, hbm, hbm,
        ],
        out_specs=(vmem, smem),
        scratch_shapes=[
            pltpu.VMEM((8, 4, ROWS, WA), BF16),
            pltpu.VMEM((8, 4, ROWS, WB + EXTRA + WC), BF16),
            pltpu.VMEM((8, 4, 4, ROWS, WC), BF16),
            pltpu.VMEM((D, 512), BF16),
            pltpu.VMEM((2, PADDED, 1024), BF16),
            pltpu.VMEM((8, 4, 2 * SLOTS, 128), BF16),
            pltpu.VMEM((8, 128, 256), BF16),
            pltpu.VMEM((8, 2, 4, ROWS, PADDED), BF16),
            pltpu.VMEM((8, 2, 2, HALF, PADDED), BF16),
            pltpu.VMEM((8, 2, 2, ROWS, PADDED), BF16),
            pltpu.VMEM((2, ROWS, PADDED), BF16),
            pltpu.VMEM((8, 2, ROWS, PADDED), F32),
            pltpu.VMEM((2, 8, ROWS, PADDED), BF16),
            pltpu.VMEM((2, 8, ROWS, PADDED), BF16),
            pltpu.VMEM((8, 128), F32),
            pltpu.VMEM((8, 128), F32),
            sem((6,)),
            sem((2,)), sem((2,)),
            sem((4,)), sem((4,)),
            sem((4,)), sem((4,)),
            sem((4,)), sem((4,)),
            sem, sem((8, 4)),
            sem((9,)), sem((9,)),
            sem, sem((8, 4)),
            sem((4,)), sem((8, 4)),
            sem, sem((8, 4)),
            sem, sem((8, 2)),
            sem, sem((8, 2)),
            sem((2, 8)), sem((2, 8)),
            sem, sem,
        ],
        compiler_params=pltpu.CompilerParams(
            collective_id=0, has_side_effects=True, vmem_limit_bytes=60 * 1024 * 1024
        ),
        cost_estimate=pl.CostEstimate(
            flops=6_000_000_000, bytes_accessed=4_000_000, transcendentals=300_000
        ),
    )(
        tokens,
        expert_ids.T,
        router_gates.T,
        replica_plan,
        w_gate,
        w_up,
        w_down.reshape(4, 2, EIGHTH, 128),
    )
    return mixed, load


def solution(mesh):
    placed = (
        P("expert", None),
        P("expert", None),
        P("expert", None),
        P(),
        P("expert", None, "dp"),
        P("expert", None, "dp"),
        P("expert", None, "dp"),
    )
    return jax.shard_map(
        per_device,
        mesh=mesh,
        in_specs=placed,
        out_specs=(P("expert", "dp"), P("expert")),
        check_vma=False,
    )
```

```python
import jax
import jax.numpy as jnp
from jax import lax
from jax.experimental import pallas as pl
from jax.experimental.pallas import tpu as pltpu
from jax.sharding import PartitionSpec as P

BF16, F32 = jnp.bfloat16, jnp.float32
ROWS, HALF = 32, 16
D = 3584
WC = 128
WA = 1536
WB = D - WA - 4 * WC
EXTRA = 128
SLOTS = 32
CAP = 4
SLABS = 8
QUARTER, EIGHTH, PADDED = 896, 448, 512


def kernel(
    tokens, ids, gates, plan, w_gate, w_up, w_down,
    out, load,
    buf_a, buf_b, buf_c, wgu, wd, hid, pt, part, xin1, xin2, xin3, xr, zin, zout, cnt, cnt_in,
    loc, w_s, w_r, wd_s, wd_r, wf_s, wf_r, ax_s, ax_r, az_s, az_r, bz_s, bz_r, bx_s, bx_r,
    cc_s, cc_r, h_s, h_r, x1_s, x1_r, x2_s, x2_r, z_s, z_r, c_s, c_r,
):
    dp = lax.axis_index("dp")
    ex = lax.axis_index("expert")
    y, zh = lax.div(dp, 2), lax.rem(dp, 2)
    x, zl, core = lax.div(ex, 16), lax.rem(lax.div(ex, 2), 8), lax.rem(ex, 2)
    z = zh * 8 + zl

    known = {}

    def at_x(dx):
        if ("x", dx) not in known:
            known["x", dx] = (dp, ex + (lax.rem(x + dx + 4, 4) - x) * 16)
        return known["x", dx]

    def at_y(dy):
        if ("y", dy) not in known:
            known["y", dy] = (lax.rem(y + dy, 4) * 2 + zh, ex)
        return known["y", dy]

    def at_z(dz):
        if ("z", dz) not in known:
            new = lax.rem(z + dz + 16, 16)
            known["z", dz] = (y * 2 + lax.div(new, 8), ex + (lax.rem(new, 8) - zl) * 2)
        return known["z", dz]

    peer = (dp, ex + 1 - 2 * core)

    def send(src, dst, ss, rs, dev):
        pltpu.make_async_remote_copy(
            src_ref=src, dst_ref=dst, send_sem=ss, recv_sem=rs, device_id=dev,
            device_id_type=pl.DeviceIdType.MESH,
        ).start()

    def arrived(ref, sem):
        pltpu.make_async_remote_copy(
            src_ref=ref, dst_ref=ref, send_sem=sem, recv_sem=sem, device_id=peer,
            device_id_type=pl.DeviceIdType.MESH,
        ).wait_recv()

    def sent(ref, sem):
        pltpu.make_async_remote_copy(
            src_ref=ref, dst_ref=ref, send_sem=sem, recv_sem=sem, device_id=peer,
            device_id_type=pl.DeviceIdType.MESH,
        ).wait_send()

    blocks = [lax.rem(x + step, 4) for step in (0, 3, 1, 2)]
    quarters = [lax.rem(y - k + 4, 4) for k in range(4)]

    def xs(q):
        return blocks[q]

    def wrap(place):
        place = jnp.where(place < 0, place + 8, place)
        return jnp.where(place >= 8, place - 8, place)

    def label(d, side):
        return wrap(zl + (2 * side - 1) * d)

    def turn_of(d, side):
        return 2 * d - 1 + side

    low, high = pl.ds(0, HALF), pl.ds(HALF, HALF)
    core_lanes = pl.multiple_of(core * 256, 128)

    own_a, own_b = buf_a.at[zl, x], buf_b.at[zl, x]
    local = [
        pltpu.make_async_copy(tokens.at[:, pl.ds(0, WA)], own_a, loc.at[0]),
        pltpu.make_async_copy(tokens.at[:, pl.ds(WA, WB)], own_b.at[:, pl.ds(0, WB)], loc.at[1]),
        pltpu.make_async_copy(w_gate.at[0], wgu.at[:, pl.ds(core_lanes, 128)], loc.at[2]),
        pltpu.make_async_copy(w_up.at[0], wgu.at[:, pl.ds(core_lanes + 128, 128)], loc.at[3]),
        pltpu.make_async_copy(
            w_down.at[y],
            wd.at[:, pl.ds(0, EIGHTH), pl.ds(pl.multiple_of((core * 4 + y) * 128, 128), 128)],
            loc.at[4],
        ),
        pltpu.make_async_copy(
            tokens.at[:, pl.ds(pl.multiple_of(WA + WB + y * WC, 128), WC)],
            own_b.at[:, pl.ds(WB + EXTRA, WC)],
            loc.at[5],
        ),
    ]
    for copy in local:
        copy.start()

    barrier = pltpu.get_barrier_semaphore()
    partners = [at_x(1), at_x(-1), at_x(2)]
    partners += [at_z(step) for step in (1, -1, 2, -2, 3, -3, 4, -4)]
    partners += [at_y(1), at_y(2), at_y(3), peer]
    for dev in partners:
        pl.semaphore_signal(barrier, inc=1, device_id=dev, device_id_type=pl.DeviceIdType.MESH)

    wd[:, pl.ds(EIGHTH, PADDED - EIGHTH), :] = jnp.zeros((2, PADDED - EIGHTH, 1024), BF16)
    cnt[...] = jnp.zeros_like(cnt)
    local[0].wait()
    pl.semaphore_wait(barrier, len(partners))

    def send_az(dist, side, q):
        way = 1 - 2 * side
        ref = buf_a.at[wrap(zl - way * (dist - 1)), xs(q)]
        jd = jnp.minimum(turn_of(dist, side), 7)
        send(ref, ref, az_s, az_r.at[jd, q], at_z(way))

    def send_bz(dist, side, rows, sem):
        way = 1 - 2 * side
        ref = buf_b.at[wrap(zl - way * (dist - 1)), x, rows]
        send(ref, ref, bz_s.at[sem], bz_r.at[sem], at_z(way))

    def send_bx(d, side):
        ref, j = buf_b.at[label(d, side), x], turn_of(d, side)
        send(ref, ref, bx_s, bx_r.at[j, 0], at_x(1))
        send(ref, ref, bx_s, bx_r.at[j, 1], at_x(-1))

    whole = pl.ds(0, ROWS)
    send(own_a, own_a, ax_s.at[0], ax_r.at[0], at_x(1))
    send(own_a, own_a, ax_s.at[1], ax_r.at[1], at_x(-1))
    send_az(1, 0, 0)
    send_az(1, 1, 0)
    for i, src in enumerate((w_gate, w_up)):
        dst = wgu.at[:, pl.ds(core_lanes + 128 * i, 128)]
        send(src.at[0], dst, w_s.at[i], w_r.at[i], peer)

    def wd_lanes(row_block, which):
        return wd.at[
            :, pl.ds(0, EIGHTH), pl.ds(pl.multiple_of((which * 4 + row_block) * 128, 128), 128)
        ]

    for k in (1, 2, 3):
        send(
            w_down.at[lax.rem(y + k, 4)], wd_lanes(y, core), wd_s.at[k], wd_r.at[k], at_y(k)
        )

    part_row = lax.broadcasted_iota(jnp.int32, (EXTRA, ROWS), 0)
    expert_row = jnp.where(part_row >= 64, part_row - 64, part_row)
    chosen = jnp.zeros((EXTRA, ROWS), F32)
    weight = jnp.zeros((EXTRA, ROWS), F32)
    for k in range(8):
        hit = ids[k : k + 1, :] == expert_row
        chosen = chosen + jnp.where(hit, 1.0, 0.0)
        weight = weight + jnp.where(hit, gates[k : k + 1, :], 0.0)
    row = lax.broadcasted_iota(jnp.int32, (ROWS, ROWS), 0)
    col = lax.broadcasted_iota(jnp.int32, (ROWS, ROWS), 1)
    earlier = ((row < col) & (((col - row) & 1) == 0)).astype(BF16)
    before = jnp.dot(chosen.astype(BF16), earlier, preferred_element_type=F32)
    weight = jnp.where(before < CAP - 0.5, weight, 0.0)
    coarse = weight.astype(BF16).astype(F32)
    parts = jnp.where(part_row < 64, coarse, weight - coarse).astype(BF16)
    buf_b[zl, x, :, pl.ds(WB, EXTRA)] = lax.dot_general(
        (row == col).astype(BF16), parts, (((1,), (1,)), ((), ())), preferred_element_type=F32
    ).astype(BF16)
    local[1].wait()
    local[5].wait()
    send_bz(1, 0, whole, 1)
    send_bz(1, 1, whole, 2)
    send_bx(0, 1)

    def first_x():
        ref = buf_a.at[zl, xs(1)]
        arrived(ref, ax_r.at[0])
        send(ref.at[low], ref.at[low], ax_s.at[2], ax_r.at[2], at_x(1))
        send_az(1, 0, 1)
        send_az(1, 1, 1)
        ref = buf_a.at[zl, xs(2)]
        arrived(ref, ax_r.at[1])
        send(ref.at[high], ref.at[high], ax_s.at[3], ax_r.at[3], at_x(-1))
        send_az(1, 0, 2)
        send_az(1, 1, 2)
        ahead_z(1, 0)
        ahead_z(1, 1)
        arrived(buf_a.at[zl, xs(3), low], ax_r.at[2])
        arrived(buf_a.at[zl, xs(3), high], ax_r.at[3])
        send_az(1, 0, 3)
        send_az(1, 1, 3)

    def along_z(d, q):
        for side in range(2):
            mine = q // 2 == side

            @pl.when((d <= 3) | mine)
            def _():
                jd = jnp.minimum(turn_of(d, side), 7)
                arrived(buf_a.at[label(d, side), xs(q)], az_r.at[jd, q])

                @pl.when((d <= 2) | ((d == 3) & mine))
                def _():
                    send_az(d + 1, side, q)

    def ahead_z(dist, side):
        half = high if side else low

        @pl.when(dist <= 3)
        def _():
            jd = turn_of(dist, side)
            arrived(buf_b.at[label(dist, side), x], bz_r.at[jd])

            @pl.when(dist <= 2)
            def _():
                send_bz(dist + 1, side, whole, jd + 2)

            @pl.when(dist == 3)
            def _():
                send_bz(4, side, half, 7 + side)

            send_bx(dist, side)

        @pl.when(dist == 4)
        def _():
            arrived(buf_b.at[label(4, side), x, half], bz_r.at[7 + side])
            if side:
                send_bx(4, 0)

    def along_x(d, side):
        slab, j = label(d, side), turn_of(d, side)
        ref = buf_b.at[slab, xs(1)]
        arrived(ref, bx_r.at[j, 0])
        send(ref.at[low], ref.at[low], bx_s, bx_r.at[j, 2], at_x(1))
        ref = buf_b.at[slab, xs(2)]
        arrived(ref, bx_r.at[j, 1])
        send(ref.at[high], ref.at[high], bx_s, bx_r.at[j, 3], at_x(-1))

    def along_x_far(d, side):
        slab, j = label(d, side), turn_of(d, side)
        arrived(buf_b.at[slab, xs(3), low], bx_r.at[j, 2])
        arrived(buf_b.at[slab, xs(3), high], bx_r.at[j, 3])
        for k in (1, 2, 3):
            send(
                buf_b.at[slab, :, :, pl.ds(WB + EXTRA, WC)], buf_c.at[slab, y],
                cc_s.at[k], cc_r.at[j, k], at_y(k),
            )

    def experts(d, side):
        slab, j = label(d, side), turn_of(d, side)
        @pl.when(j == 0)
        def _():
            local[2].wait()
            local[3].wait()
            other = pl.multiple_of((1 - core) * 256, 128)
            for i in range(2):
                arrived(wgu.at[:, pl.ds(other + 128 * i, 128)], w_r.at[i])

        acc = jnp.dot(
            buf_a[slab].reshape(128, WA), wgu[pl.ds(0, WA), :], preferred_element_type=F32
        )
        acc = acc + jnp.dot(
            buf_b[slab, :, :, pl.ds(0, WB)].reshape(128, WB),
            wgu[pl.ds(WA, WB), :],
            preferred_element_type=F32,
        )

        def quarter(which):
            return wgu[pl.ds(pl.multiple_of(WA + WB + which * WC, WC), WC), :]

        acc = acc + jnp.dot(
            buf_b[slab, :, :, pl.ds(WB + EXTRA, WC)].reshape(128, WC),
            quarter(y),
            preferred_element_type=F32,
        )
        for k in (1, 2, 3):
            which = quarters[k]
            arrived(buf_c.at[slab, which], cc_r.at[j, k])
            acc = acc + jnp.dot(
                buf_c[slab, which].reshape(128, WC), quarter(which), preferred_element_type=F32
            )
        mix = buf_b[slab, :, :, pl.ds(WB, EXTRA)].reshape(128, EXTRA)
        lane = lax.broadcasted_iota(jnp.int32, (EXTRA, 256), 0)
        unit = lax.broadcasted_iota(jnp.int32, (EXTRA, 256), 1)
        wanted = (ex - core) + (unit >= 128).astype(jnp.int32)
        pick = ((lane == wanted) | (lane == wanted + 64)).astype(BF16)
        scale = jnp.dot(mix, pick, preferred_element_type=F32)
        gate_out = jnp.concatenate([acc[:, 0:128], acc[:, 256:384]], axis=1)
        up_out = jnp.concatenate([acc[:, 128:256], acc[:, 384:512]], axis=1)
        hidden = gate_out / (1.0 + jnp.exp(-gate_out)) * up_out * scale
        hidden = hidden.astype(BF16)
        row = lax.broadcasted_iota(jnp.int32, (128, 128), 0)
        col = lax.broadcasted_iota(jnp.int32, (128, 128), 1)
        earlier = (col < row) & ((row >> 5) == (col >> 5)) & (((row - col) & 1) == 0)
        token = lax.broadcasted_iota(jnp.int32, (128, 256), 0)
        slot = lax.broadcasted_iota(jnp.int32, (128, 256), 1) & 127
        first = ((token >> 5) * 8 + (token & 1) * 4).astype(F32)
        served = jnp.where(scale > 0.0, 1.0, 0.0)
        before = jnp.dot(earlier.astype(BF16), served.astype(BF16), preferred_element_type=F32)
        place = jnp.where(before + first == slot.astype(F32), served, 0.0).astype(BF16)
        pt[slab] = place
        for e in range(2):
            lanes = slice(e * 128, e * 128 + 128)
            packed = lax.dot_general(
                place[:, lanes], hidden[:, lanes], (((0,), (0,)), ((), ())),
                preferred_element_type=F32,
            )
            hid[slab, y, pl.ds(e * SLOTS, SLOTS), :] = packed[0:SLOTS].astype(BF16)
        for k in (1, 2, 3):
            ref = hid.at[slab, y]
            send(ref, ref, h_s, h_r.at[j, k], at_y(k))
        kept = jnp.where(mix.astype(F32) > 0.0, 1.0, 0.0).astype(BF16)
        r = lax.broadcasted_iota(jnp.int32, (8, 128), 0)
        t = lax.broadcasted_iota(jnp.int32, (8, 128), 1)
        parity = (r == (t & 1)).astype(BF16)
        cnt[...] += jnp.dot(parity, kept, preferred_element_type=F32)

    def pass_down_weights():
        local[4].wait()
        ref = wd_lanes(y, core)
        send(ref, ref, wf_s.at[0], wf_r.at[0], peer)
        for k in (1, 2, 3):
            ref = wd_lanes(quarters[k], core)
            arrived(ref, wd_r.at[k])
            send(ref, ref, wf_s.at[k], wf_r.at[k], peer)

    def down(d, side):
        slab, j = label(d, side), turn_of(d, side)
        @pl.when(j == 0)
        def _():
            for k in range(4):
                arrived(wd_lanes(quarters[k], 1 - core), wf_r.at[k])

        for k in (1, 2, 3):
            arrived(hid.at[slab, quarters[k]], h_r.at[j, k])
        spread = []
        for e in range(2):
            rows = pl.ds(e * SLOTS, SLOTS)
            packed = jnp.concatenate([hid[slab, i, rows, :] for i in range(4)], axis=1)
            place = pt[slab, :, pl.ds(e * 128, 128)][:, 0:SLOTS]
            spread.append(jnp.dot(place, packed, preferred_element_type=F32).astype(BF16))
        joined = jnp.concatenate(spread, axis=1)
        for side in range(2):
            value = lax.dot_general(
                joined, wd[side], (((1,), (1,)), ((), ())), preferred_element_type=F32
            )
            part[slab, side] = value.astype(BF16).reshape(4, ROWS, PADDED)
        far = part.at[slab, :, xs(3)]

        @pl.when(j < 5)
        def _():
            send(far.at[:, low], xin1.at[j, 0], x1_s, x1_r.at[j, 0], at_x(1))
            send(far.at[:, high], xin1.at[j, 1], x1_s, x1_r.at[j, 1], at_x(-1))

        @pl.when(j >= 5)
        def _():
            send(far, xin3.at[j - 5], x1_s, x1_r.at[j, 0], at_x(2))
            send(part.at[slab, :, xs(2)], xin2.at[j, 0], x2_s, x2_r.at[j, 0], at_x(1))
            send(part.at[slab, :, xs(1)], xin2.at[j, 1], x2_s, x2_r.at[j, 1], at_x(-1))

    def add_far(d, side):
        slab, j = label(d, side), turn_of(d, side)
        for i, (q, rows, step) in enumerate(((2, low, 1), (1, high, -1))):
            arrived(xin1.at[j, i], x1_r.at[j, i])
            there = part[slab, :, xs(q), rows, :].astype(F32) + xin1[j, i].astype(F32)
            part[slab, :, xs(q), rows, :] = there.astype(BF16)
            send(part.at[slab, :, xs(q)], xin2.at[j, i], x2_s, x2_r.at[j, i], at_x(step))

    halves = {
        (side, s): lax.div(lax.rem(z + (1 - 2 * side) * (8 - s) + 16, 16), 8)
        for side in range(2)
        for s in range(8)
    }

    def z_step(s, way, side, kind):
        slab = wrap(zl - s * way)
        half = halves[side, s]
        value = xr[slab, half]
        rows = low if side == 0 else high
        if kind == "first":
            zout[side, s] = value.astype(BF16)
            send(
                zout.at[side, s, rows], zin.at[side, s, rows],
                z_s.at[side, s], z_r.at[side, s], at_z(way),
            )
            return
        if kind == "second":
            arrived(zin.at[side, s - 1, rows], z_r.at[side, s - 1])
            zout[side, s] = value.astype(BF16)
            more = xr[slab, half, rows, :] + zin[side, s - 1, rows, :].astype(F32)
            zout[side, s, rows, :] = more.astype(BF16)
        elif kind == "alone":
            zout[side, s] = value.astype(BF16)
        else:
            arrived(zin.at[side, s - 1], z_r.at[side, s - 1])
            zout[side, s] = (value + zin[side, s - 1].astype(F32)).astype(BF16)
        there = at_z(way if kind in ("second", "on") else (8 - s) * way)
        send(zout.at[side, s], zin.at[side, s], z_s.at[side, s], z_r.at[side, s], there)

    def both(s, kind):
        z_step(s, 1, 0, kind)
        z_step(s, -1, 1, kind)

    def add_near(d, side):
        slab, j = label(d, side), turn_of(d, side)
        arrived(xin2.at[j, 0], x2_r.at[j, 0])
        arrived(xin2.at[j, 1], x2_r.at[j, 1])
        xr[slab] = (
            part[slab, :, x].astype(F32) + xin2[j, 0].astype(F32) + xin2[j, 1].astype(F32)
        )

        @pl.when(j >= 5)
        def _():
            arrived(xin3.at[j - 5], x1_r.at[j, 0])
            xr[slab] = xr[slab] + xin3[j - 5].astype(F32)

    def send_c(j):
        for k in (1, 2, 3):
            send(
                buf_b.at[slab, :, :, pl.ds(WB + EXTRA, WC)], buf_c.at[slab, y],
                cc_s.at[k], cc_r.at[j, k], at_y(k),
            )

    def pair(d, work):
        def one(side, carry):
            work(d, side)
            return carry

        lax.fori_loop(0, 2, one, 0)

    def slabs(d, work, least=0, most=4):
        @pl.when((d >= max(least, 1)) & (d <= most))
        def _():
            work(d, 0)

        @pl.when((d >= least) & (d <= min(most, 3)))
        def _():
            work(d, 1)

    def loop_slabs(d, work):
        def one(side, carry):
            work(d, side)
            return carry

        lax.fori_loop(jnp.where(d == 0, 1, 0), jnp.where(d == 4, 1, 2), one, 0)

    def turn(d, carry):
        @pl.when(d == 0)
        def _():
            first_x()

        for q in range(4):

            @pl.when(d >= 1)
            def _():
                along_z(d, q)

            if q == 0:

                @pl.when(d >= 1)
                def _():
                    along_x(d, 0)

            if q == 1:

                @pl.when(d <= 3)
                def _():
                    along_x(d, 1)

            if q >= 2:

                @pl.when(d <= 2)
                def _():
                    ahead_z(d + 2, q - 2)

            if q == 2:

                @pl.when(d >= 1)
                def _():
                    loop_slabs(d - 1, experts)

                @pl.when(d == 1)
                def _():
                    pass_down_weights()

            if q == 3:
                slabs(d, along_x_far)

                @pl.when(d >= 3)
                def _():
                    loop_slabs(d - 3, add_near)

                    @pl.when(d == 3)
                    def _():
                        both(0, "first")

                    @pl.when(d == 4)
                    def _():
                        both(1, "second")
                        both(7, "alone")

                @pl.when(d >= 2)
                def _():
                    loop_slabs(d - 2, add_far)

        @pl.when(d >= 1)
        def _():
            loop_slabs(d - 1, down)

        return carry

    lax.fori_loop(0, 5, turn, 0)
    experts(4, 0)
    send(cnt, cnt_in, c_s, c_r, peer)
    pair(2, add_near)
    both(2, "on")
    both(6, "alone")
    down(4, 0)
    pair(3, add_near)
    both(3, "on")
    both(5, "alone")
    add_near(4, 0)
    both(4, "straight")

    arrived(cnt_in, c_r)
    total = cnt[...] + cnt_in[...]
    r = lax.broadcasted_iota(jnp.int32, (8, 128), 0)
    t = lax.broadcasted_iota(jnp.int32, (8, 128), 1)
    copied = plan[ex]
    served = ((r == 0) & (t == ex)) | ((r == 1) & (t == copied))
    load[0] = jnp.sum(jnp.where(served, total, 0.0)) * (1.0 / 256.0)

    block_a, block_b = buf_a.at[0, 0], buf_b.at[0, 0]
    sent(block_a, ax_s.at[0])
    sent(block_a, ax_s.at[1])
    sent(block_a.at[low], ax_s.at[2])
    sent(block_a.at[low], ax_s.at[3])
    sent(block_b.at[low], bz_s.at[7])
    sent(block_b.at[low], bz_s.at[8])
    for jd in range(1, 7):
        sent(block_b, bz_s.at[jd])
    sent(buf_a.at[pl.ds(0, 7)], az_s)
    sent(buf_b.at[pl.ds(0, 6)], bx_s)
    sent(wd.at[0, pl.ds(0, 192)], h_s)
    for k in (1, 2, 3):
        sent(wd.at[0, pl.ds(0, WC)], cc_s.at[k])
    sent(wd.at[0, pl.ds(0, 256)], x1_s)
    sent(wd.at[0], x2_s)
    sent(w_gate.at[0], w_s.at[0])
    sent(w_up.at[0], w_s.at[1])
    sent(cnt, c_s)
    sent(wd_lanes(0, 0), wf_s.at[0])
    for k in (1, 2, 3):
        sent(w_down.at[0], wd_s.at[k])
        sent(wd_lanes(0, 0), wf_s.at[k])
    for side in range(2):
        sent(zout.at[side, 0, low], z_s.at[side, 0])
        for step in range(1, 8):
            sent(zout.at[side, step], z_s.at[side, step])

    mixed = xr[zl, zh]
    for step in (7, 6, 5, 4):
        for side in range(2):
            arrived(zin.at[side, step], z_r.at[side, step])
            mixed = mixed + zin[side, step].astype(F32)
    out[...] = mixed[:, 0:EIGHTH].astype(BF16)


def per_device(tokens, expert_ids, router_gates, replica_plan, w_gate, w_up, w_down):
    hbm = pl.BlockSpec(memory_space=pltpu.HBM)
    smem = pl.BlockSpec(memory_space=pltpu.SMEM)
    vmem = pl.BlockSpec(memory_space=pltpu.VMEM)
    sem = pltpu.SemaphoreType.DMA
    mixed, load = pl.pallas_call(
        kernel,
        out_shape=(
            jax.ShapeDtypeStruct((ROWS, EIGHTH), BF16),
            jax.ShapeDtypeStruct((1,), F32),
        ),
        in_specs=[
            hbm, vmem, vmem, smem, hbm, hbm, hbm,
        ],
        out_specs=(vmem, smem),
        scratch_shapes=[
            pltpu.VMEM((8, 4, ROWS, WA), BF16),
            pltpu.VMEM((8, 4, ROWS, WB + EXTRA + WC), BF16),
            pltpu.VMEM((8, 4, 4, ROWS, WC), BF16),
            pltpu.VMEM((D, 512), BF16),
            pltpu.VMEM((2, PADDED, 1024), BF16),
            pltpu.VMEM((8, 4, 2 * SLOTS, 128), BF16),
            pltpu.VMEM((8, 128, 256), BF16),
            pltpu.VMEM((8, 2, 4, ROWS, PADDED), BF16),
            pltpu.VMEM((8, 2, 2, HALF, PADDED), BF16),
            pltpu.VMEM((8, 2, 2, ROWS, PADDED), BF16),
            pltpu.VMEM((3, 2, ROWS, PADDED), BF16),
            pltpu.VMEM((8, 2, ROWS, PADDED), F32),
            pltpu.VMEM((2, 8, ROWS, PADDED), BF16),
            pltpu.VMEM((2, 8, ROWS, PADDED), BF16),
            pltpu.VMEM((8, 128), F32),
            pltpu.VMEM((8, 128), F32),
            sem((6,)),
            sem((2,)), sem((2,)),
            sem((4,)), sem((4,)),
            sem((4,)), sem((4,)),
            sem((4,)), sem((4,)),
            sem, sem((8, 4)),
            sem((9,)), sem((9,)),
            sem, sem((8, 4)),
            sem((4,)), sem((8, 4)),
            sem, sem((8, 4)),
            sem, sem((8, 2)),
            sem, sem((8, 2)),
            sem((2, 8)), sem((2, 8)),
            sem, sem,
        ],
        compiler_params=pltpu.CompilerParams(
            collective_id=0, has_side_effects=True, vmem_limit_bytes=60 * 1024 * 1024
        ),
        cost_estimate=pl.CostEstimate(
            flops=6_000_000_000, bytes_accessed=4_000_000, transcendentals=300_000
        ),
    )(
        tokens,
        expert_ids.T,
        router_gates.T,
        replica_plan,
        w_gate,
        w_up,
        w_down.reshape(4, 2, EIGHTH, 128),
    )
    return mixed, load


def solution(mesh):
    placed = (
        P("expert", None),
        P("expert", None),
        P("expert", None),
        P(),
        P("expert", None, "dp"),
        P("expert", None, "dp"),
        P("expert", None, "dp"),
    )
    return jax.shard_map(
        per_device,
        mesh=mesh,
        in_specs=placed,
        out_specs=(P("expert", "dp"), P("expert")),
        check_vma=False,
    )
```

```python
import jax
import jax.numpy as jnp
from jax import lax
from jax.experimental import pallas as pl
from jax.experimental.pallas import tpu as pltpu
from jax.sharding import PartitionSpec as P

BF16, F32 = jnp.bfloat16, jnp.float32
ROWS, HALF = 32, 16
D = 3584
WC = 128
WA = 1408
WB = D - WA - 4 * WC
EXTRA = 128
SLOTS = 32
CAP = 4
SLABS = 8
QUARTER, EIGHTH, PADDED = 896, 448, 512


def kernel(
    tokens, ids, gates, plan, w_gate, w_up, w_down,
    out, load,
    buf_a, buf_b, buf_c, wgu, wd, hid, pt, part, xin1, xin2, xin3, xr, zin, zout, cnt, cnt_in,
    loc, w_s, w_r, wd_s, wd_r, wf_s, wf_r, ax_s, ax_r, az_s, az_r, bz_s, bz_r, bx_s, bx_r,
    cc_s, cc_r, h_s, h_r, x1_s, x1_r, x2_s, x2_r, z_s, z_r, c_s, c_r,
):
    dp = lax.axis_index("dp")
    ex = lax.axis_index("expert")
    y, zh = lax.div(dp, 2), lax.rem(dp, 2)
    x, zl, core = lax.div(ex, 16), lax.rem(lax.div(ex, 2), 8), lax.rem(ex, 2)
    z = zh * 8 + zl

    known = {}

    def at_x(dx):
        if ("x", dx) not in known:
            known["x", dx] = (dp, ex + (lax.rem(x + dx + 4, 4) - x) * 16)
        return known["x", dx]

    def at_y(dy):
        if ("y", dy) not in known:
            known["y", dy] = (lax.rem(y + dy, 4) * 2 + zh, ex)
        return known["y", dy]

    def at_z(dz):
        if ("z", dz) not in known:
            new = lax.rem(z + dz + 16, 16)
            known["z", dz] = (y * 2 + lax.div(new, 8), ex + (lax.rem(new, 8) - zl) * 2)
        return known["z", dz]

    peer = (dp, ex + 1 - 2 * core)

    def send(src, dst, ss, rs, dev):
        pltpu.make_async_remote_copy(
            src_ref=src, dst_ref=dst, send_sem=ss, recv_sem=rs, device_id=dev,
            device_id_type=pl.DeviceIdType.MESH,
        ).start()

    def arrived(ref, sem):
        pltpu.make_async_remote_copy(
            src_ref=ref, dst_ref=ref, send_sem=sem, recv_sem=sem, device_id=peer,
            device_id_type=pl.DeviceIdType.MESH,
        ).wait_recv()

    def sent(ref, sem):
        pltpu.make_async_remote_copy(
            src_ref=ref, dst_ref=ref, send_sem=sem, recv_sem=sem, device_id=peer,
            device_id_type=pl.DeviceIdType.MESH,
        ).wait_send()

    blocks = [lax.rem(x + step, 4) for step in (0, 3, 1, 2)]
    quarters = [lax.rem(y - k + 4, 4) for k in range(4)]

    def xs(q):
        return blocks[q]

    def wrap(place):
        place = jnp.where(place < 0, place + 8, place)
        return jnp.where(place >= 8, place - 8, place)

    def label(d, side):
        return wrap(zl + (2 * side - 1) * d)

    def turn_of(d, side):
        return 2 * d - 1 + side

    low, high = pl.ds(0, HALF), pl.ds(HALF, HALF)
    core_lanes = pl.multiple_of(core * 256, 128)

    own_a, own_b = buf_a.at[zl, x], buf_b.at[zl, x]
    local = [
        pltpu.make_async_copy(tokens.at[:, pl.ds(0, WA)], own_a, loc.at[0]),
        pltpu.make_async_copy(tokens.at[:, pl.ds(WA, WB)], own_b.at[:, pl.ds(0, WB)], loc.at[1]),
        pltpu.make_async_copy(w_gate.at[0], wgu.at[:, pl.ds(core_lanes, 128)], loc.at[2]),
        pltpu.make_async_copy(w_up.at[0], wgu.at[:, pl.ds(core_lanes + 128, 128)], loc.at[3]),
        pltpu.make_async_copy(
            w_down.at[y],
            wd.at[:, pl.ds(0, EIGHTH), pl.ds(pl.multiple_of((core * 4 + y) * 128, 128), 128)],
            loc.at[4],
        ),
        pltpu.make_async_copy(
            tokens.at[:, pl.ds(pl.multiple_of(WA + WB + y * WC, 128), WC)],
            own_b.at[:, pl.ds(WB + EXTRA, WC)],
            loc.at[5],
        ),
    ]
    for copy in local:
        copy.start()

    barrier = pltpu.get_barrier_semaphore()
    partners = [at_x(1), at_x(-1), at_x(2)]
    partners += [at_z(step) for step in (1, -1, 2, -2, 3, -3, 4, -4)]
    partners += [at_y(1), at_y(2), at_y(3), peer]
    for dev in partners:
        pl.semaphore_signal(barrier, inc=1, device_id=dev, device_id_type=pl.DeviceIdType.MESH)

    wd[:, pl.ds(EIGHTH, PADDED - EIGHTH), :] = jnp.zeros((2, PADDED - EIGHTH, 1024), BF16)
    cnt[...] = jnp.zeros_like(cnt)
    local[0].wait()
    pl.semaphore_wait(barrier, len(partners))

    def send_az(dist, side, q):
        way = 1 - 2 * side
        ref = buf_a.at[wrap(zl - way * (dist - 1)), xs(q)]
        jd = jnp.minimum(turn_of(dist, side), 7)
        send(ref, ref, az_s, az_r.at[jd, q], at_z(way))

    def send_bz(dist, side, rows, sem):
        way = 1 - 2 * side
        ref = buf_b.at[wrap(zl - way * (dist - 1)), x, rows]
        send(ref, ref, bz_s.at[sem], bz_r.at[sem], at_z(way))

    def send_bx(d, side):
        ref, j = buf_b.at[label(d, side), x], turn_of(d, side)
        send(ref, ref, bx_s, bx_r.at[j, 0], at_x(1))
        send(ref, ref, bx_s, bx_r.at[j, 1], at_x(-1))

    whole = pl.ds(0, ROWS)
    send(own_a, own_a, ax_s.at[0], ax_r.at[0], at_x(1))
    send(own_a, own_a, ax_s.at[1], ax_r.at[1], at_x(-1))
    send_az(1, 0, 0)
    send_az(1, 1, 0)
    for i, src in enumerate((w_gate, w_up)):
        dst = wgu.at[:, pl.ds(core_lanes + 128 * i, 128)]
        send(src.at[0], dst, w_s.at[i], w_r.at[i], peer)

    def wd_lanes(row_block, which):
        return wd.at[
            :, pl.ds(0, EIGHTH), pl.ds(pl.multiple_of((which * 4 + row_block) * 128, 128), 128)
        ]

    for k in (1, 2, 3):
        send(
            w_down.at[lax.rem(y + k, 4)], wd_lanes(y, core), wd_s.at[k], wd_r.at[k], at_y(k)
        )

    part_row = lax.broadcasted_iota(jnp.int32, (EXTRA, ROWS), 0)
    expert_row = jnp.where(part_row >= 64, part_row - 64, part_row)
    chosen = jnp.zeros((EXTRA, ROWS), F32)
    weight = jnp.zeros((EXTRA, ROWS), F32)
    for k in range(8):
        hit = ids[k : k + 1, :] == expert_row
        chosen = chosen + jnp.where(hit, 1.0, 0.0)
        weight = weight + jnp.where(hit, gates[k : k + 1, :], 0.0)
    row = lax.broadcasted_iota(jnp.int32, (ROWS, ROWS), 0)
    col = lax.broadcasted_iota(jnp.int32, (ROWS, ROWS), 1)
    earlier = ((row < col) & (((col - row) & 1) == 0)).astype(BF16)
    before = jnp.dot(chosen.astype(BF16), earlier, preferred_element_type=F32)
    weight = jnp.where(before < CAP - 0.5, weight, 0.0)
    coarse = weight.astype(BF16).astype(F32)
    parts = jnp.where(part_row < 64, coarse, weight - coarse).astype(BF16)
    buf_b[zl, x, :, pl.ds(WB, EXTRA)] = lax.dot_general(
        (row == col).astype(BF16), parts, (((1,), (1,)), ((), ())), preferred_element_type=F32
    ).astype(BF16)
    local[1].wait()
    local[5].wait()
    send_bz(1, 0, whole, 1)
    send_bz(1, 1, whole, 2)
    send_bx(0, 1)

    def first_x():
        ref = buf_a.at[zl, xs(1)]
        arrived(ref, ax_r.at[0])
        send(ref.at[low], ref.at[low], ax_s.at[2], ax_r.at[2], at_x(1))
        send_az(1, 0, 1)
        send_az(1, 1, 1)
        ref = buf_a.at[zl, xs(2)]
        arrived(ref, ax_r.at[1])
        send(ref.at[high], ref.at[high], ax_s.at[3], ax_r.at[3], at_x(-1))
        send_az(1, 0, 2)
        send_az(1, 1, 2)
        ahead_z(1, 0)
        ahead_z(1, 1)
        arrived(buf_a.at[zl, xs(3), low], ax_r.at[2])
        arrived(buf_a.at[zl, xs(3), high], ax_r.at[3])
        send_az(1, 0, 3)
        send_az(1, 1, 3)

    def along_z(d, q):
        for side in range(2):
            mine = q // 2 == side

            @pl.when((d <= 3) | mine)
            def _():
                jd = jnp.minimum(turn_of(d, side), 7)
                arrived(buf_a.at[label(d, side), xs(q)], az_r.at[jd, q])

                @pl.when((d <= 2) | ((d == 3) & mine))
                def _():
                    send_az(d + 1, side, q)

    def ahead_z(dist, side):
        half = high if side else low

        @pl.when(dist <= 3)
        def _():
            jd = turn_of(dist, side)
            arrived(buf_b.at[label(dist, side), x], bz_r.at[jd])

            @pl.when(dist <= 2)
            def _():
                send_bz(dist + 1, side, whole, jd + 2)

            @pl.when(dist == 3)
            def _():
                send_bz(4, side, half, 7 + side)

            send_bx(dist, side)

        @pl.when(dist == 4)
        def _():
            arrived(buf_b.at[label(4, side), x, half], bz_r.at[7 + side])
            if side:
                send_bx(4, 0)

    def along_x(d, side):
        slab, j = label(d, side), turn_of(d, side)
        ref = buf_b.at[slab, xs(1)]
        arrived(ref, bx_r.at[j, 0])
        send(ref.at[low], ref.at[low], bx_s, bx_r.at[j, 2], at_x(1))
        ref = buf_b.at[slab, xs(2)]
        arrived(ref, bx_r.at[j, 1])
        send(ref.at[high], ref.at[high], bx_s, bx_r.at[j, 3], at_x(-1))

    def along_x_far(d, side):
        slab, j = label(d, side), turn_of(d, side)
        arrived(buf_b.at[slab, xs(3), low], bx_r.at[j, 2])
        arrived(buf_b.at[slab, xs(3), high], bx_r.at[j, 3])
        for k in (1, 2, 3):
            send(
                buf_b.at[slab, :, :, pl.ds(WB + EXTRA, WC)], buf_c.at[slab, y],
                cc_s.at[k], cc_r.at[j, k], at_y(k),
            )

    def experts(d, side):
        slab, j = label(d, side), turn_of(d, side)
        @pl.when(j == 0)
        def _():
            local[2].wait()
            local[3].wait()
            other = pl.multiple_of((1 - core) * 256, 128)
            for i in range(2):
                arrived(wgu.at[:, pl.ds(other + 128 * i, 128)], w_r.at[i])

        acc = jnp.dot(
            buf_a[slab].reshape(128, WA), wgu[pl.ds(0, WA), :], preferred_element_type=F32
        )
        acc = acc + jnp.dot(
            buf_b[slab, :, :, pl.ds(0, WB)].reshape(128, WB),
            wgu[pl.ds(WA, WB), :],
            preferred_element_type=F32,
        )

        def quarter(which):
            return wgu[pl.ds(pl.multiple_of(WA + WB + which * WC, WC), WC), :]

        acc = acc + jnp.dot(
            buf_b[slab, :, :, pl.ds(WB + EXTRA, WC)].reshape(128, WC),
            quarter(y),
            preferred_element_type=F32,
        )
        for k in (1, 2, 3):
            which = quarters[k]
            arrived(buf_c.at[slab, which], cc_r.at[j, k])
            acc = acc + jnp.dot(
                buf_c[slab, which].reshape(128, WC), quarter(which), preferred_element_type=F32
            )
        mix = buf_b[slab, :, :, pl.ds(WB, EXTRA)].reshape(128, EXTRA)
        lane = lax.broadcasted_iota(jnp.int32, (EXTRA, 256), 0)
        unit = lax.broadcasted_iota(jnp.int32, (EXTRA, 256), 1)
        wanted = (ex - core) + (unit >= 128).astype(jnp.int32)
        pick = ((lane == wanted) | (lane == wanted + 64)).astype(BF16)
        scale = jnp.dot(mix, pick, preferred_element_type=F32)
        gate_out = jnp.concatenate([acc[:, 0:128], acc[:, 256:384]], axis=1)
        up_out = jnp.concatenate([acc[:, 128:256], acc[:, 384:512]], axis=1)
        hidden = gate_out / (1.0 + jnp.exp(-gate_out)) * up_out * scale
        hidden = hidden.astype(BF16)
        row = lax.broadcasted_iota(jnp.int32, (128, 128), 0)
        col = lax.broadcasted_iota(jnp.int32, (128, 128), 1)
        earlier = (col < row) & ((row >> 5) == (col >> 5)) & (((row - col) & 1) == 0)
        token = lax.broadcasted_iota(jnp.int32, (128, 256), 0)
        slot = lax.broadcasted_iota(jnp.int32, (128, 256), 1) & 127
        first = ((token >> 5) * 8 + (token & 1) * 4).astype(F32)
        served = jnp.where(scale > 0.0, 1.0, 0.0)
        before = jnp.dot(earlier.astype(BF16), served.astype(BF16), preferred_element_type=F32)
        place = jnp.where(before + first == slot.astype(F32), served, 0.0).astype(BF16)
        pt[slab] = place
        for e in range(2):
            lanes = slice(e * 128, e * 128 + 128)
            packed = lax.dot_general(
                place[:, lanes], hidden[:, lanes], (((0,), (0,)), ((), ())),
                preferred_element_type=F32,
            )
            hid[slab, y, pl.ds(e * SLOTS, SLOTS), :] = packed[0:SLOTS].astype(BF16)
        for k in (1, 2, 3):
            ref = hid.at[slab, y]
            send(ref, ref, h_s, h_r.at[j, k], at_y(k))
        kept = jnp.where(mix.astype(F32) > 0.0, 1.0, 0.0).astype(BF16)
        r = lax.broadcasted_iota(jnp.int32, (8, 128), 0)
        t = lax.broadcasted_iota(jnp.int32, (8, 128), 1)
        parity = (r == (t & 1)).astype(BF16)
        cnt[...] += jnp.dot(parity, kept, preferred_element_type=F32)

    def pass_down_weights():
        local[4].wait()
        ref = wd_lanes(y, core)
        send(ref, ref, wf_s.at[0], wf_r.at[0], peer)
        for k in (1, 2, 3):
            ref = wd_lanes(quarters[k], core)
            arrived(ref, wd_r.at[k])
            send(ref, ref, wf_s.at[k], wf_r.at[k], peer)

    def down(d, side):
        slab, j = label(d, side), turn_of(d, side)
        @pl.when(j == 0)
        def _():
            for k in range(4):
                arrived(wd_lanes(quarters[k], 1 - core), wf_r.at[k])

        for k in (1, 2, 3):
            arrived(hid.at[slab, quarters[k]], h_r.at[j, k])
        spread = []
        for e in range(2):
            rows = pl.ds(e * SLOTS, SLOTS)
            packed = jnp.concatenate([hid[slab, i, rows, :] for i in range(4)], axis=1)
            place = pt[slab, :, pl.ds(e * 128, 128)][:, 0:SLOTS]
            spread.append(jnp.dot(place, packed, preferred_element_type=F32).astype(BF16))
        joined = jnp.concatenate(spread, axis=1)
        for side in range(2):
            value = lax.dot_general(
                joined, wd[side], (((1,), (1,)), ((), ())), preferred_element_type=F32
            )
            part[slab, side] = value.astype(BF16).reshape(4, ROWS, PADDED)
        far = part.at[slab, :, xs(3)]

        @pl.when(j < 5)
        def _():
            send(far.at[:, low], xin1.at[j, 0], x1_s, x1_r.at[j, 0], at_x(1))
            send(far.at[:, high], xin1.at[j, 1], x1_s, x1_r.at[j, 1], at_x(-1))

        @pl.when(j >= 5)
        def _():
            send(far, xin3.at[j - 5], x1_s, x1_r.at[j, 0], at_x(2))
            send(part.at[slab, :, xs(2)], xin2.at[j, 0], x2_s, x2_r.at[j, 0], at_x(1))
            send(part.at[slab, :, xs(1)], xin2.at[j, 1], x2_s, x2_r.at[j, 1], at_x(-1))

    def add_far(d, side):
        slab, j = label(d, side), turn_of(d, side)
        for i, (q, rows, step) in enumerate(((2, low, 1), (1, high, -1))):
            arrived(xin1.at[j, i], x1_r.at[j, i])
            there = part[slab, :, xs(q), rows, :].astype(F32) + xin1[j, i].astype(F32)
            part[slab, :, xs(q), rows, :] = there.astype(BF16)
            send(part.at[slab, :, xs(q)], xin2.at[j, i], x2_s, x2_r.at[j, i], at_x(step))

    halves = {
        (side, s): lax.div(lax.rem(z + (1 - 2 * side) * (8 - s) + 16, 16), 8)
        for side in range(2)
        for s in range(8)
    }

    def z_step(s, way, side, kind):
        slab = wrap(zl - s * way)
        half = halves[side, s]
        value = xr[slab, half]
        rows = low if side == 0 else high
        if kind == "first":
            zout[side, s] = value.astype(BF16)
            send(
                zout.at[side, s, rows], zin.at[side, s, rows],
                z_s.at[side, s], z_r.at[side, s], at_z(way),
            )
            return
        if kind == "second":
            arrived(zin.at[side, s - 1, rows], z_r.at[side, s - 1])
            zout[side, s] = value.astype(BF16)
            more = xr[slab, half, rows, :] + zin[side, s - 1, rows, :].astype(F32)
            zout[side, s, rows, :] = more.astype(BF16)
        elif kind == "alone":
            zout[side, s] = value.astype(BF16)
        else:
            arrived(zin.at[side, s - 1], z_r.at[side, s - 1])
            zout[side, s] = (value + zin[side, s - 1].astype(F32)).astype(BF16)
        there = at_z(way if kind in ("second", "on") else (8 - s) * way)
        send(zout.at[side, s], zin.at[side, s], z_s.at[side, s], z_r.at[side, s], there)

    def both(s, kind):
        z_step(s, 1, 0, kind)
        z_step(s, -1, 1, kind)

    def add_near(d, side):
        slab, j = label(d, side), turn_of(d, side)
        arrived(xin2.at[j, 0], x2_r.at[j, 0])
        arrived(xin2.at[j, 1], x2_r.at[j, 1])
        xr[slab] = (
            part[slab, :, x].astype(F32) + xin2[j, 0].astype(F32) + xin2[j, 1].astype(F32)
        )

        @pl.when(j >= 5)
        def _():
            arrived(xin3.at[j - 5], x1_r.at[j, 0])
            xr[slab] = xr[slab] + xin3[j - 5].astype(F32)

    def send_c(j):
        for k in (1, 2, 3):
            send(
                buf_b.at[slab, :, :, pl.ds(WB + EXTRA, WC)], buf_c.at[slab, y],
                cc_s.at[k], cc_r.at[j, k], at_y(k),
            )

    def pair(d, work):
        def one(side, carry):
            work(d, side)
            return carry

        lax.fori_loop(0, 2, one, 0)

    def slabs(d, work, least=0, most=4):
        @pl.when((d >= max(least, 1)) & (d <= most))
        def _():
            work(d, 0)

        @pl.when((d >= least) & (d <= min(most, 3)))
        def _():
            work(d, 1)

    def loop_slabs(d, work):
        def one(side, carry):
            work(d, side)
            return carry

        lax.fori_loop(jnp.where(d == 0, 1, 0), jnp.where(d == 4, 1, 2), one, 0)

    def turn(d, carry):
        @pl.when(d == 0)
        def _():
            first_x()

        for q in range(4):

            @pl.when(d >= 1)
            def _():
                along_z(d, q)

            if q == 0:

                @pl.when(d >= 1)
                def _():
                    along_x(d, 0)

            if q == 1:

                @pl.when(d <= 3)
                def _():
                    along_x(d, 1)

            if q >= 2:

                @pl.when(d <= 2)
                def _():
                    ahead_z(d + 2, q - 2)

            if q == 2:

                @pl.when(d >= 1)
                def _():
                    loop_slabs(d - 1, experts)

                @pl.when(d == 1)
                def _():
                    pass_down_weights()

            if q == 3:
                slabs(d, along_x_far)

                @pl.when(d >= 3)
                def _():
                    loop_slabs(d - 3, add_near)

                    @pl.when(d == 3)
                    def _():
                        both(0, "first")

                    @pl.when(d == 4)
                    def _():
                        both(1, "second")
                        both(7, "alone")

                @pl.when(d >= 2)
                def _():
                    loop_slabs(d - 2, add_far)

        @pl.when(d >= 1)
        def _():
            loop_slabs(d - 1, down)

        return carry

    lax.fori_loop(0, 5, turn, 0)
    experts(4, 0)
    send(cnt, cnt_in, c_s, c_r, peer)
    pair(2, add_near)
    both(2, "on")
    both(6, "alone")
    down(4, 0)
    pair(3, add_near)
    both(3, "on")
    both(5, "alone")
    add_near(4, 0)
    both(4, "straight")

    arrived(cnt_in, c_r)
    total = cnt[...] + cnt_in[...]
    r = lax.broadcasted_iota(jnp.int32, (8, 128), 0)
    t = lax.broadcasted_iota(jnp.int32, (8, 128), 1)
    copied = plan[ex]
    served = ((r == 0) & (t == ex)) | ((r == 1) & (t == copied))
    load[0] = jnp.sum(jnp.where(served, total, 0.0)) * (1.0 / 256.0)

    block_a, block_b = buf_a.at[0, 0], buf_b.at[0, 0]
    sent(block_a, ax_s.at[0])
    sent(block_a, ax_s.at[1])
    sent(block_a.at[low], ax_s.at[2])
    sent(block_a.at[low], ax_s.at[3])
    sent(block_b.at[low], bz_s.at[7])
    sent(block_b.at[low], bz_s.at[8])
    for jd in range(1, 7):
        sent(block_b, bz_s.at[jd])
    sent(buf_a.at[pl.ds(0, 7)], az_s)
    sent(buf_b.at[pl.ds(0, 6)], bx_s)
    sent(wd.at[0, pl.ds(0, 192)], h_s)
    for k in (1, 2, 3):
        sent(wd.at[0, pl.ds(0, WC)], cc_s.at[k])
    sent(wd.at[0, pl.ds(0, 256)], x1_s)
    sent(wd.at[0], x2_s)
    sent(w_gate.at[0], w_s.at[0])
    sent(w_up.at[0], w_s.at[1])
    sent(cnt, c_s)
    sent(wd_lanes(0, 0), wf_s.at[0])
    for k in (1, 2, 3):
        sent(w_down.at[0], wd_s.at[k])
        sent(wd_lanes(0, 0), wf_s.at[k])
    for side in range(2):
        sent(zout.at[side, 0, low], z_s.at[side, 0])
        for step in range(1, 8):
            sent(zout.at[side, step], z_s.at[side, step])

    mixed = xr[zl, zh]
    for step in (7, 6, 5, 4):
        for side in range(2):
            arrived(zin.at[side, step], z_r.at[side, step])
            mixed = mixed + zin[side, step].astype(F32)
    out[...] = mixed[:, 0:EIGHTH].astype(BF16)


def per_device(tokens, expert_ids, router_gates, replica_plan, w_gate, w_up, w_down):
    hbm = pl.BlockSpec(memory_space=pltpu.HBM)
    smem = pl.BlockSpec(memory_space=pltpu.SMEM)
    vmem = pl.BlockSpec(memory_space=pltpu.VMEM)
    sem = pltpu.SemaphoreType.DMA
    mixed, load = pl.pallas_call(
        kernel,
        out_shape=(
            jax.ShapeDtypeStruct((ROWS, EIGHTH), BF16),
            jax.ShapeDtypeStruct((1,), F32),
        ),
        in_specs=[
            hbm, vmem, vmem, smem, hbm, hbm, hbm,
        ],
        out_specs=(vmem, smem),
        scratch_shapes=[
            pltpu.VMEM((8, 4, ROWS, WA), BF16),
            pltpu.VMEM((8, 4, ROWS, WB + EXTRA + WC), BF16),
            pltpu.VMEM((8, 4, 4, ROWS, WC), BF16),
            pltpu.VMEM((D, 512), BF16),
            pltpu.VMEM((2, PADDED, 1024), BF16),
            pltpu.VMEM((8, 4, 2 * SLOTS, 128), BF16),
            pltpu.VMEM((8, 128, 256), BF16),
            pltpu.VMEM((8, 2, 4, ROWS, PADDED), BF16),
            pltpu.VMEM((8, 2, 2, HALF, PADDED), BF16),
            pltpu.VMEM((8, 2, 2, ROWS, PADDED), BF16),
            pltpu.VMEM((3, 2, ROWS, PADDED), BF16),
            pltpu.VMEM((8, 2, ROWS, PADDED), F32),
            pltpu.VMEM((2, 8, ROWS, PADDED), BF16),
            pltpu.VMEM((2, 8, ROWS, PADDED), BF16),
            pltpu.VMEM((8, 128), F32),
            pltpu.VMEM((8, 128), F32),
            sem((6,)),
            sem((2,)), sem((2,)),
            sem((4,)), sem((4,)),
            sem((4,)), sem((4,)),
            sem((4,)), sem((4,)),
            sem, sem((8, 4)),
            sem((9,)), sem((9,)),
            sem, sem((8, 4)),
            sem((4,)), sem((8, 4)),
            sem, sem((8, 4)),
            sem, sem((8, 2)),
            sem, sem((8, 2)),
            sem((2, 8)), sem((2, 8)),
            sem, sem,
        ],
        compiler_params=pltpu.CompilerParams(
            collective_id=0, has_side_effects=True, vmem_limit_bytes=60 * 1024 * 1024
        ),
        cost_estimate=pl.CostEstimate(
            flops=6_000_000_000, bytes_accessed=4_000_000, transcendentals=300_000
        ),
    )(
        tokens,
        expert_ids.T,
        router_gates.T,
        replica_plan,
        w_gate,
        w_up,
        w_down.reshape(4, 2, EIGHTH, 128),
    )
    return mixed, load


def solution(mesh):
    placed = (
        P("expert", None),
        P("expert", None),
        P("expert", None),
        P(),
        P("expert", None, "dp"),
        P("expert", None, "dp"),
        P("expert", None, "dp"),
    )
    return jax.shard_map(
        per_device,
        mesh=mesh,
        in_specs=placed,
        out_specs=(P("expert", "dp"), P("expert")),
        check_vma=False,
    )
```
